256 devices in a mesh: expert: 8 (over z), tensor: 32 (over x, y, core).
Axes of the slice: x: 4, y: 4, z: 8, core: 2. Of those that a mesh axis runs over, the one named last changes fastest.
Arguments:
- tokens: bfloat16 [1024, 7168], P('expert', 'tensor'), may hold values from -48 to 48
- norm_gain: float32 [7168], replicated, may hold values from 0.25 to 1.75
- route_ids: int32 [1024, 2], P('expert'), may hold values from 0 to 7, all different within a row; in each aligned block of 128 rows (0 to 127, 128 to 255, ...) at most 48 rows name the same one
- route_probs: float32 [1024, 2], P('expert'), may hold values from 0.2 to 1
- dense_gate: bfloat16 [4864, 7168], P('tensor'), may hold values from -0.0625 to 0.0625
- dense_up: bfloat16 [4864, 7168], P('tensor'), may hold values from -0.0625 to 0.0625
- dense_down: bfloat16 [4864, 7168], P('tensor'), may hold values from -0.15625 to 0.15625
- expert_gate: bfloat16 [8, 4864, 7168], P('expert', 'tensor'), may hold values from -0.0625 to 0.0625
- expert_up: bfloat16 [8, 4864, 7168], P('expert', 'tensor'), may hold values from -0.0625 to 0.0625
- expert_down: bfloat16 [8, 4864, 7168], P('expert', 'tensor'), may hold values from -0.15625 to 0.15625
Outputs:
- block_out: bfloat16 [1024, 7168], P('expert', 'tensor')
The draws below stay inside these ranges and needn't reach their ends.
Inputs may be any that keep to these rules, and one draw needn't show every extreme that they name: `route_ids`: in each aligned block of 128 rows (the rows of one index of the expert axis) no expert is named by more than 48 rows, a bound that some block reaches; the 2 ids of a row differ.
All inputs are finite; a program needn't handle non-finite values.
Results may differ from the reference program's by a relative error of at most 0.0064.
Values may be sent and summed in bfloat16 or wider, within the bound.
No kernel may reach another device: no remote copies, remote signals or barrier semaphores. Data moves between devices by JAX's collectives and lax.ppermute only.
A program may use at most 128 MiB of HBM per device.

```python
import math
import jax
import jax.numpy as jnp
import numpy as np
from jax import lax

D = 7168
FF = 4864
EFF = 4864
TOP = 2
TOK_DEV = 128
EXPERTS = 8
CAP = 48
TOKENS = 1024
N_EXPERT = 8


def draw_tokens(key, part):
    key = jax.random.fold_in(key, 11)
    first, second, third = jax.random.split(key, 3)
    row_scale = jnp.exp(jax.random.uniform(second, (TOKENS, 1), jnp.float32, math.log(0.3), math.log(3.0)))
    col_scale = jnp.exp(jax.random.uniform(third, (1, D), jnp.float32, math.log(0.4), math.log(4.0)))
    base = jnp.clip(jax.random.normal(first, (TOKENS, D), jnp.float32), -4.0, 4.0)
    return (base * row_scale * col_scale).astype(jnp.bfloat16)


def strengthened(entries, rng, source, target, parts, factor):
    def block_of(dim):
        return (jnp.arange(entries.shape[dim]) // (entries.shape[dim] // parts)).reshape((-1,) + (1,) * (entries.ndim - 1 - dim))

    one_side = jax.random.permutation(rng, parts)[block_of(target)]
    far = (block_of(target) + parts // 2) % parts
    return jnp.where((block_of(source) == one_side) | (block_of(source) == far), factor * entries, entries)


def level_of(key, extent, cuts, least, largest):
    loudness = 1.0
    for dim, shards_of in cuts:
        steps = jax.random.uniform(jax.random.fold_in(jax.random.fold_in(key, 6), dim), (shards_of,), jnp.float32, least / len(cuts), largest / len(cuts))
        loudness = loudness * jnp.repeat(jnp.exp(steps), extent[dim] // shards_of).reshape((-1,) + (1,) * (len(extent) - 1 - dim))
    return loudness


def deal_out(key, own, number, rows, amount, top, bound, lean):
    sequence = jax.random.permutation(key, amount)
    packed, usual = shares(amount, rows * top, bound, lean, True), shares(amount, rows * top, bound, lean, False)
    places = jnp.arange(amount)

    def named(lengths, turn):
        used = int((lengths > 0).sum())
        fixed = max(1, used // 4)
        shifted = fixed + (places - fixed + turn * (used - fixed)) % max(1, amount - fixed)
        return jnp.zeros((amount,), jnp.int32).at[sequence[jnp.where(places < fixed, places, shifted)]].set(jnp.asarray(lengths, jnp.int32))

    lengths = jnp.where(number % 4 == 0, named(packed, number // 4), named(usual, number - number // 4 - 1))
    mixed = jax.random.permutation(jax.random.fold_in(own, 3), amount)
    giver, receiver = mixed[0:amount // 2 * 2:2], mixed[1:amount // 2 * 2:2]
    room = jnp.minimum(lengths[giver] - 1, bound - lengths[receiver]) // 2
    room = jnp.where((giver == sequence[0]) | (receiver == sequence[0]) | (lengths[receiver] == 0), 0, jnp.maximum(room, 0))
    shifted = jax.random.randint(jax.random.fold_in(own, 4), (amount // 2,), 0, 1 << 20) % (room + 1)
    lengths = lengths.at[giver].add(-shifted).at[receiver].add(shifted)
    members = jnp.searchsorted(jnp.cumsum(lengths), jnp.arange(rows * top), side="right").astype(jnp.int32)
    table = members.reshape(top, rows).T
    table = table[jax.random.permutation(jax.random.fold_in(own, 1), rows)]
    turn = jax.random.randint(jax.random.fold_in(own, 2), (rows, 1), 0, top)
    return jnp.take_along_axis(table, (jnp.arange(top)[None, :] + turn) % top, axis=1)


def shares(amount, total, bound, skew, full):
    loads = [(1 << 20) // math.isqrt(standing ** skew) + 1 for standing in range(1, amount + 1)]
    largest = bound if full else min(bound, max(-(-total // amount), total * loads[0] // sum(loads)))
    least = 1 if total - largest >= amount - 1 else 0
    holding, spare = [largest] + [least] * (amount - 1), total - largest - least * (amount - 1)
    while spare > 0:
        free = [i for i in range(1, amount) if holding[i] < largest] or [i for i in range(1, amount) if holding[i] < bound]
        whole, budget = sum([loads[i] for i in free]), spare
        for i in free:
            addition = min(bound - holding[i], max(1, budget * loads[i] // whole), spare)
            holding[i] = holding[i] + addition
            spare = spare - addition
    return np.array(holding)


def scatter_about(own_key, shape, spread, most, cuts=(), dtype=jnp.bfloat16):
    entries = spread * jax.random.normal(own_key, shape, jnp.float32)
    if cuts:
        entries = entries * level_of(own_key, shape, cuts, -0.22, 0.18)
    return jnp.clip(entries, -most, most).astype(dtype)


def bell_draw_with(key, extent, deviation, bound, cuts, heavy, kind=jnp.bfloat16):
    result = deviation * jax.random.normal(key, extent, jnp.float32)
    if cuts:
        result = result * level_of(key, extent, cuts, -0.22, 0.18)
    return jnp.clip(strengthened(result, jax.random.fold_in(key, 3), *heavy), -bound, bound).astype(kind)


def setup_inputs(seed: int = 0) -> dict:
    keys = jax.random.split(jax.random.key(seed), 11)
    tokens = draw_tokens(jax.random.fold_in(keys[10], 71), 0)
    norm_gain = jnp.clip(1.0 + 0.15 * jax.random.normal(keys[1], (D,), jnp.float32), 0.25, 1.75)
    route_ids_keys = jax.random.split(jax.random.fold_in(keys[2], 1), TOKENS // TOK_DEV)
    route_ids_turns = jax.random.permutation(jax.random.fold_in(keys[2], 3), TOKENS // TOK_DEV)
    route_ids = jax.vmap(lambda own, number: deal_out(jax.random.fold_in(keys[2], 2), own, number, TOK_DEV, EXPERTS, TOP, CAP, 2))(route_ids_keys, route_ids_turns).reshape((TOKENS, TOP))
    route_probs = jnp.clip(0.2 + 0.8 * jax.random.uniform(keys[3], (TOKENS, TOP), jnp.float32) ** level_of(keys[3], (TOKENS, TOP), ((0, 8),), -0.2, 0.2), 0.2, 1.0)
    dense_gate = scatter_about(keys[4], (FF, D), D ** -0.5, 0.0625, ((0, 32),))
    dense_up = scatter_about(keys[5], (FF, D), D ** -0.5, 0.0625, ((0, 32),))
    dense_down = bell_draw_with(keys[6], (FF, D), FF ** -0.5, 0.15625, ((0, 32),), (0, 1, 32, 2.75))
    expert_gate = scatter_about(keys[7], (EXPERTS, EFF, D), D ** -0.5, 0.0625, ((0, 8), (1, 32)))
    expert_up = scatter_about(keys[8], (EXPERTS, EFF, D), D ** -0.5, 0.0625, ((0, 8), (1, 32)))
    expert_down = bell_draw_with(keys[9], (EXPERTS, EFF, D), EFF ** -0.5, 0.15625, ((0, 8), (1, 32)), (1, 2, 32, 2.75))
    return dict(tokens=tokens, norm_gain=norm_gain, route_ids=route_ids, route_probs=route_probs, dense_gate=dense_gate, dense_up=dense_up, dense_down=dense_down, expert_gate=expert_gate, expert_up=expert_up, expert_down=expert_down)


def rms_normed(tokens, norm_gain):
    values = tokens.astype(jnp.float32)
    scale = lax.rsqrt(lax.optimization_barrier(jnp.mean(values * values, axis=-1, keepdims=True)) + 1e-05)
    return (values * scale * norm_gain.astype(jnp.float32)).astype(jnp.bfloat16)

def reference(tokens, norm_gain, route_ids, route_probs, dense_gate, dense_up, dense_down, expert_gate, expert_up, expert_down):
    normed = rms_normed(tokens, norm_gain)
    gate_proj = jnp.dot(normed, dense_gate.T, preferred_element_type=jnp.float32)
    up_proj = jnp.dot(normed, dense_up.T, preferred_element_type=jnp.float32)
    dense_hidden = (jax.nn.silu(gate_proj) * up_proj).astype(jnp.bfloat16)
    dense_out = jnp.dot(dense_hidden, dense_down, preferred_element_type=jnp.float32)
    row_limit = N_EXPERT * CAP

    def one_expert(expert_index, moe_out):
        matched = route_ids == expert_index
        weight = lax.optimization_barrier(jnp.sum(jnp.where(matched, route_probs, 0.0), axis=1))
        chosen = jnp.any(matched, axis=1)
        picked_index = jnp.nonzero(chosen, size=row_limit, fill_value=0)[0]
        usable = jnp.arange(row_limit) < jnp.sum(chosen.astype(jnp.int32))
        picked = normed[picked_index]
        gate_rows = jnp.dot(picked, expert_gate[expert_index].T, preferred_element_type=jnp.float32)
        up_rows = jnp.dot(picked, expert_up[expert_index].T, preferred_element_type=jnp.float32)
        expert_hidden = (jax.nn.silu(gate_rows) * up_rows).astype(jnp.bfloat16)
        expert_out = jnp.dot(expert_hidden, expert_down[expert_index], preferred_element_type=jnp.float32)
        factor = jnp.where(usable, weight[picked_index], 0.0)
        return moe_out.at[picked_index].add(expert_out * factor[:, None])
    moe_out = lax.fori_loop(0, EXPERTS, one_expert, jnp.zeros(dense_out.shape, jnp.float32))
    return (dense_out + moe_out).astype(jnp.bfloat16)
```

```python
import functools

import jax
import jax.numpy as jnp
from jax import lax
from jax.experimental import pallas as pl
from jax.experimental.pallas import tpu as pltpu
from jax.sharding import PartitionSpec as P

SIDE = 4
PAIR = 2
CHIPS = SIDE * SIDE
VMEM = pltpu.MemorySpace.VMEM
SMEM = pltpu.MemorySpace.SMEM


def device_of(x, y, core):
    return (x * SIDE + y) * PAIR + core


def hops(step, first):
    pairs = []
    for x in range(SIDE):
        for y in range(SIDE):
            for core in range(PAIR):
                along_x = (core == 0) == first
                to_x = (x + step) % SIDE if along_x else x
                to_y = y if along_x else (y + step) % SIDE
                pairs.append((device_of(x, y, core), device_of(to_x, to_y, core)))
    return pairs


def sibling(value):
    return lax.ppermute(value, "tensor", [(i, i ^ 1) for i in range(CHIPS * PAIR)])


def chip_back(x, y, core, outer, inner):
    back_x = jnp.where(core == 0, inner, outer)
    back_y = jnp.where(core == 0, outer, inner)
    return lax.rem(x - back_x + SIDE, SIDE), lax.rem(y - back_y + SIDE, SIDE)


def hidden_kernel(dense_rows, place, *refs):
    stacks, refs = refs[: 2 * SIDE], refs[2 * SIDE :]
    gain, dense_gate, dense_up, expert_gate, expert_up, hidden, whole, arrived = refs
    x, y, core = place[0], place[1], place[2]
    cols = stacks[0].shape[1]
    width, rows = whole.shape
    copies = []
    for half in range(2):
        owner = core if half == 0 else 1 - core
        for outer in range(SIDE):
            for inner in range(SIDE):
                from_x, from_y = chip_back(x, y, owner, outer, inner)
                index = device_of(from_x, from_y, owner)
                copies.append(
                    pltpu.make_async_copy(
                        stacks[half * SIDE + outer].at[inner],
                        whole.at[pl.ds(pl.multiple_of(index * cols, 16), cols), :],
                        arrived.at[len(copies)],
                    )
                )
    for copy in copies:
        copy.start()
    for copy in copies:
        copy.wait()

    def squares(i, total):
        block = whole[pl.ds(pl.multiple_of(i * 32, 32), 32), :].astype(jnp.float32)
        block = block * block
        return total + jnp.sum(block.reshape(4, 8, rows), axis=0)

    total = lax.fori_loop(0, width // 32, squares, jnp.zeros((8, rows), jnp.float32), unroll=8)
    scale = lax.rsqrt(jnp.sum(total, axis=0, keepdims=True) / width + 1e-05)
    chunk = 896

    def product(weight, at, normed):
        return jnp.dot(weight[:, at], normed, preferred_element_type=jnp.float32)

    def step(k, sums):
        at = pl.ds(pl.multiple_of(k * chunk, chunk), chunk)
        gains = jnp.concatenate([gain[at, :]] * (rows // 128), axis=1)
        normed = (whole[at, :].astype(jnp.float32) * scale * gains).astype(jnp.bfloat16)
        dense, routed = normed[:, :dense_rows], normed[:, dense_rows:]
        return (
            sums[0] + product(dense_gate, at, dense),
            sums[1] + product(dense_up, at, dense),
            sums[2] + product(expert_gate, at, routed),
            sums[3] + product(expert_up, at, routed),
        )

    units = dense_gate.shape[0]
    zeros = lambda n: jnp.zeros((units, n), jnp.float32)
    sums = lax.fori_loop(
        0,
        width // chunk,
        step,
        (zeros(dense_rows), zeros(dense_rows), zeros(rows - dense_rows), zeros(rows - dense_rows)),
    )
    for gates, ups, span in (
        (sums[0], sums[1], slice(0, dense_rows)),
        (sums[2], sums[3], slice(dense_rows, rows)),
    ):
        hidden[:, span] = (gates / (1.0 + jnp.exp(-gates)) * ups).astype(jnp.bfloat16)


def hidden_units(place, stacks, gain, dense_gate, dense_up, expert_gate, expert_up, dense_rows):
    cols, rows = stacks[0].shape[1:]
    width = CHIPS * PAIR * cols
    in_vmem = pl.BlockSpec(memory_space=VMEM)
    return pl.pallas_call(
        functools.partial(hidden_kernel, dense_rows),
        out_shape=jax.ShapeDtypeStruct((dense_gate.shape[0], rows), jnp.bfloat16),
        in_specs=[pl.BlockSpec(memory_space=SMEM)]
        + [pl.BlockSpec(memory_space=pl.ANY)] * len(stacks)
        + [in_vmem] * 5,
        out_specs=in_vmem,
        scratch_shapes=[
            pltpu.VMEM((width, rows), jnp.bfloat16),
            pltpu.SemaphoreType.DMA((CHIPS * PAIR,)),
        ],
        compiler_params=pltpu.CompilerParams(vmem_limit_bytes=40 * 1024 * 1024),
        cost_estimate=pl.CostEstimate(
            flops=4 * dense_gate.shape[0] * rows * width, bytes_accessed=16 << 20, transcendentals=0
        ),
        name="hidden_units",
    )(place, *stacks, gain, dense_gate, dense_up, expert_gate, expert_up)


def down_kernel(dense_rows, place, hidden, *refs):
    for half in range(2):
        dense, routed, out = refs[2 * half], refs[2 * half + 1], refs[4 + half]
        for weight, span in (
            (dense, slice(0, dense_rows)),
            (routed, slice(dense_rows, hidden.shape[1])),
        ):
            out[0, :, span] = jnp.dot(
                weight[...], hidden[:, span], preferred_element_type=jnp.float32
            ).astype(jnp.bfloat16)


def down_pieces(place, hidden, dense_down, expert_down, outer, cols, dense_rows):
    units, rows = hidden.shape

    def block(half):
        def index(inner, place):
            x, y, core = place[0], place[1], place[2]
            owner = core if half == 0 else 1 - core
            to_x = lax.rem(x + jnp.where(owner == 0, inner, outer), SIDE)
            to_y = lax.rem(y + jnp.where(owner == 0, outer, inner), SIDE)
            return device_of(to_x, to_y, owner), 0

        return pl.BlockSpec((cols, units), index)

    out = pl.BlockSpec((1, cols, rows), lambda inner, place: (inner, 0, 0))
    shape = jax.ShapeDtypeStruct((SIDE, cols, rows), jnp.bfloat16)
    return pl.pallas_call(
        functools.partial(down_kernel, dense_rows),
        out_shape=(shape, shape),
        grid_spec=pltpu.PrefetchScalarGridSpec(
            num_scalar_prefetch=1,
            grid=(SIDE,),
            in_specs=[
                pl.BlockSpec((units, rows), lambda inner, place: (0, 0)),
                block(0),
                block(0),
                block(1),
                block(1),
            ],
            out_specs=(out, out),
        ),
        compiler_params=pltpu.CompilerParams(vmem_limit_bytes=16 * 1024 * 1024),
        cost_estimate=pl.CostEstimate(
            flops=4 * SIDE * cols * rows * units, bytes_accessed=4 << 20, transcendentals=0
        ),
        name=f"down_pieces_{outer}",
    )(place, hidden, dense_down, expert_down, dense_down, expert_down)


def shards(
    tokens,
    norm_gain,
    route_ids,
    route_probs,
    dense_gate,
    dense_up,
    dense_down,
    expert_gate,
    expert_up,
    expert_down,
):
    f32, bf16 = jnp.float32, jnp.bfloat16
    experts = lax.axis_size("expert")
    tok_rows, choose = route_ids.shape
    cols = tokens.shape[1]
    capacity = 3 * tok_rows * choose // (2 * experts)
    index = lax.axis_index("tensor")
    core = index % PAIR
    place = jnp.stack([index // (SIDE * PAIR), index // PAIR % SIDE, core]).astype(jnp.int32)

    flat_ids = route_ids.reshape(-1)
    onehot = (flat_ids[:, None] == jnp.arange(experts, dtype=jnp.int32)[None, :]).astype(jnp.int32)
    position = jnp.sum((jnp.cumsum(onehot, axis=0) - 1) * onehot, axis=1)
    slot_ids = (flat_ids * capacity + position).reshape(tok_rows, choose)
    slot_hits = (
        jnp.arange(experts * capacity, dtype=jnp.int32)[:, None, None] == slot_ids[None, :, :]
    )
    dispatch = jnp.any(slot_hits, axis=2).astype(bf16)
    combine = jnp.sum(jnp.where(slot_hits, route_probs[None, :, :], 0.0), axis=2)

    outgoing = jnp.dot(dispatch, tokens, preferred_element_type=f32).astype(bf16)
    received = lax.all_to_all(
        outgoing.reshape(experts, capacity, cols), "expert", 0, 0, tiled=True
    ).reshape(experts * capacity, cols)
    own = jnp.concatenate([tokens.T, received.T], axis=1)

    first = [own] + [lax.ppermute(own, "tensor", hops(d, True)) for d in range(1, SIDE)]
    stack = jnp.stack(first)
    stacks = [stack] + [lax.ppermute(stack, "tensor", hops(d, False)) for d in range(1, SIDE)]
    others = [sibling(part) for part in stacks]

    gain = jnp.broadcast_to(norm_gain[:, None], (norm_gain.shape[0], 128))
    hidden = hidden_units(
        place, stacks + others, gain, dense_gate, dense_up, expert_gate[0], expert_up[0], tok_rows
    )

    dense_down, routed_down = dense_down.T, expert_down[0].T
    pieces = {}
    for outer in (1, 2, 3, 0):
        mine, others = down_pieces(place, hidden, dense_down, routed_down, outer, cols, tok_rows)
        pieces[outer] = mine.astype(f32) + sibling(others).astype(f32)
    level = pieces[0]
    for d in range(1, SIDE):
        level = level + lax.ppermute(pieces[d].astype(bf16), "tensor", hops(d, False)).astype(f32)
    total = level[0]
    for d in range(1, SIDE):
        total = total + lax.ppermute(level[d].astype(bf16), "tensor", hops(d, True)).astype(f32)

    back = total[:, tok_rows:].T.reshape(experts, capacity, cols)
    returned = lax.all_to_all(back, "expert", 0, 0, tiled=True).reshape(experts * capacity, cols)
    moe_out = jnp.dot(combine.T, returned, precision=lax.Precision.HIGHEST)
    return (total[:, :tok_rows].T + moe_out).astype(bf16)


def solution(mesh):
    in_specs = (
        P("expert", "tensor"),
        P(),
        P("expert", None),
        P("expert", None),
        P("tensor", None),
        P("tensor", None),
        P("tensor", None),
        P("expert", "tensor", None),
        P("expert", "tensor", None),
        P("expert", "tensor", None),
    )
    out_specs = P("expert", "tensor")
    return jax.shard_map(shards, mesh=mesh, in_specs=in_specs, out_specs=out_specs, check_vma=False)
```

```python
import functools

import jax
import jax.numpy as jnp
from jax import lax
from jax.experimental import pallas as pl
from jax.experimental.pallas import tpu as pltpu
from jax.sharding import PartitionSpec as P

SIDE = 4
PAIR = 2
CHIPS = SIDE * SIDE
GROUP = CHIPS * PAIR
F32 = jnp.float32
BF16 = jnp.bfloat16
MIB = 1024 * 1024


def device_of(x, y, core):
    return (x * SIDE + y) * PAIR + core


def hops(step, first):
    pairs = []
    for x in range(SIDE):
        for y in range(SIDE):
            for core in range(PAIR):
                along_x = (core == 0) == first
                to_x = (x + step) % SIDE if along_x else x
                to_y = y if along_x else (y + step) % SIDE
                pairs.append((device_of(x, y, core), device_of(to_x, to_y, core)))
    return pairs


def sibling(value):
    return lax.ppermute(value, "tensor", [(i, i ^ 1) for i in range(GROUP)])


def piece_index(place, other, sign, outer, inner):
    x, y, core = place[0], place[1], place[2]
    owner = 1 - core if other else core
    move_x = jnp.where(owner == 0, inner, outer)
    move_y = jnp.where(owner == 0, outer, inner)
    at_x = lax.rem(x + sign * move_x + SIDE, SIDE)
    at_y = lax.rem(y + sign * move_y + SIDE, SIDE)
    return device_of(at_x, at_y, owner)


def dispatch_kernel(experts, capacity, ids, probs, tokens, outgoing, combine):
    choose, rows = ids.shape
    slots = experts * capacity
    numbers = lax.broadcasted_iota(jnp.int32, (experts, rows), 0)
    before = lax.broadcasted_iota(jnp.int32, (rows, rows), 0)
    after = lax.broadcasted_iota(jnp.int32, (rows, rows), 1)
    earlier = (before < after).astype(F32).astype(BF16)
    slot_numbers = lax.broadcasted_iota(jnp.int32, (slots, rows), 0)
    taken = jnp.zeros((experts, 1), F32)
    weights = jnp.zeros((slots, rows), F32)
    chosen = jnp.zeros((slots, rows), F32)
    for k in range(choose):
        named = ids[k : k + 1, :]
        onehot = (numbers == named).astype(F32)
        ahead = jnp.dot(onehot.astype(BF16), earlier, preferred_element_type=F32) + taken
        position = jnp.sum(ahead * onehot, axis=0, keepdims=True).astype(jnp.int32)
        hits = slot_numbers == named * capacity + position
        weights = weights + jnp.where(hits, probs[k : k + 1, :], 0.0)
        chosen = chosen + hits.astype(F32)
        taken = taken + jnp.sum(onehot, axis=1, keepdims=True)
    combine[...] = weights
    outgoing[...] = lax.dot_general(
        chosen.astype(BF16), tokens[...], (((1,), (1,)), ((), ())), preferred_element_type=F32
    ).astype(BF16)


def dispatched(ids, probs, tokens, experts, capacity):
    cols, rows = tokens.shape
    return pl.pallas_call(
        functools.partial(dispatch_kernel, experts, capacity),
        out_shape=(
            jax.ShapeDtypeStruct((experts * capacity, cols), BF16),
            jax.ShapeDtypeStruct((experts * capacity, rows), F32),
        ),
        name="dispatch",
    )(ids, probs, tokens)


def weights_kernel(cols, gain, *refs):
    ins, outs = refs[:6], refs[6:]
    for i in range(ins[0].shape[1] // cols):
        at = slice(i * cols, (i + 1) * cols)
        for gate, up, out in ((ins[0], ins[1], outs[0]), (ins[2], ins[3], outs[1])):
            both = jnp.concatenate([gate[:, at].astype(F32), up[:, at].astype(F32)], axis=0)
            out[i] = (both * gain[:, at]).astype(BF16)
        for down, out in ((ins[4], outs[2]), (ins[5], outs[3])):
            out[i] = down[:, at].astype(F32).T.astype(BF16)


def piece_weights(gain, dense_gate, dense_up, expert_gate, expert_up, dense_down, expert_down, cols):
    units, width = dense_gate.shape
    each = 4
    wide = pl.BlockSpec((units, each * cols), lambda i: (0, i))
    up_shape = jax.ShapeDtypeStruct((width // cols, 2 * units, cols), BF16)
    down_shape = jax.ShapeDtypeStruct((width // cols, cols, units), BF16)
    return pl.pallas_call(
        functools.partial(weights_kernel, cols),
        out_shape=(up_shape, up_shape, down_shape, down_shape),
        grid=(width // (each * cols),),
        in_specs=[pl.BlockSpec((1, each * cols), lambda i: (0, i))] + [wide] * 6,
        out_specs=[pl.BlockSpec((each, 2 * units, cols), lambda i: (i, 0, 0))] * 2
        + [pl.BlockSpec((each, cols, units), lambda i: (i, 0, 0))] * 2,
        compiler_params=pltpu.CompilerParams(vmem_limit_bytes=56 * MIB),
        cost_estimate=pl.CostEstimate(flops=12 * units * width, bytes_accessed=28 * MIB, transcendentals=0),
        name="piece_weights",
    )(gain, dense_gate, dense_up, expert_gate, expert_up, dense_down, expert_down)


def arrive_kernel(dense_rows, count, start, last, width, place, *refs):
    stacks, refs = refs[:count], refs[count:]
    dense, routed, refs = refs[:count], refs[count : 2 * count], refs[2 * count :]
    if not start:
        carried, refs = refs[:3], refs[3:]
    if last:
        hidden, refs = refs[0], refs[1:]
    dense_sum, routed_sum, squares = refs

    @pl.when(pl.program_id(0) == 0)
    def _():
        for i, ref in enumerate((dense_sum, routed_sum, squares)):
            ref[...] = jnp.zeros_like(ref) if start else carried[i][...]

    for j in range(count):
        block = stacks[j][0]
        dense_sum[...] += jnp.dot(dense[j][0], block[:, :dense_rows], preferred_element_type=F32)
        routed_sum[...] += jnp.dot(routed[j][0], block[:, dense_rows:], preferred_element_type=F32)
        values = block.astype(F32)
        values = values * values
        squares[...] += jnp.sum(values.reshape(values.shape[0] // 8, 8, values.shape[1]), axis=0)

    if last:

        @pl.when(pl.program_id(0) == pl.num_programs(0) - 1)
        def _():
            scale = lax.rsqrt(jnp.sum(squares[...], axis=0, keepdims=True) / width + 1e-05)
            units = dense_sum.shape[0] // 2
            for sums, span in (
                (dense_sum, slice(0, dense_rows)),
                (routed_sum, slice(dense_rows, scale.shape[1])),
            ):
                gates = sums[:units, :] * scale[:, span]
                ups = sums[units:, :] * scale[:, span]
                hidden[:, span] = (gates / (1.0 + jnp.exp(-gates)) * ups).astype(BF16)


def arrive(place, stage, dense, routed, sums, dense_rows, last=False):
    count = len(stage)
    cols, rows = stage[0][0].shape[1:]
    height = dense.shape[1]
    start = sums is None

    def weight(outer, other):
        def index(i, place):
            return piece_index(place, other, -1, outer, i), 0, 0

        return pl.BlockSpec((1, height, cols), index)

    whole = lambda shape: pl.BlockSpec(shape, lambda i, place: (0, 0))
    shapes = [(height, dense_rows), (height, rows - dense_rows), (8, rows)]
    sum_specs = [whole(s) for s in shapes]
    sum_shapes = [jax.ShapeDtypeStruct(s, F32) for s in shapes]
    hidden_shape = (height // 2, rows)
    if last:
        out_specs, out_shape, scratch = (
            whole(hidden_shape),
            jax.ShapeDtypeStruct(hidden_shape, BF16),
            [pltpu.VMEM(s, F32) for s in shapes],
        )
    else:
        out_specs, out_shape, scratch = sum_specs, sum_shapes, []
    weights = [weight(outer, other) for _, outer, other in stage]
    return pl.pallas_call(
        functools.partial(arrive_kernel, dense_rows, count, start, last, GROUP * cols),
        out_shape=out_shape,
        grid_spec=pltpu.PrefetchScalarGridSpec(
            num_scalar_prefetch=1,
            grid=(SIDE,),
            in_specs=[pl.BlockSpec((1, cols, rows), lambda i, place: (i, 0, 0))] * count
            + weights * 2
            + ([] if start else sum_specs),
            out_specs=out_specs,
            scratch_shapes=scratch,
        ),
        compiler_params=pltpu.CompilerParams(vmem_limit_bytes=24 * MIB),
        cost_estimate=pl.CostEstimate(
            flops=2 * SIDE * count * height * cols * rows,
            bytes_accessed=2 * MIB * count,
            transcendentals=0,
        ),
        name=f"arrive_{stage[-1][1]}_{count}",
    )(
        place,
        *[stack for stack, _, _ in stage],
        *[dense] * count,
        *[routed] * count,
        *([] if start else sums),
    )


def down_kernel(dense_rows, place, hidden, *refs):
    for half in range(2):
        dense, routed, out = refs[2 * half], refs[2 * half + 1], refs[4 + half]
        for weight, span in (
            (dense, slice(0, dense_rows)),
            (routed, slice(dense_rows, hidden.shape[1])),
        ):
            out[0, :, span] = jnp.dot(
                weight[0], hidden[:, span], preferred_element_type=F32
            ).astype(out.dtype)


def down_pieces(place, hidden, dense_down, expert_down, outer, dense_rows):
    units, rows = hidden.shape
    cols = dense_down.shape[1]

    def weight(other):
        def index(i, place):
            return piece_index(place, other, 1, outer, i), 0, 0

        return pl.BlockSpec((1, cols, units), index)

    out = pl.BlockSpec((1, cols, rows), lambda i, place: (i, 0, 0))
    shape = (SIDE, cols, rows)
    return pl.pallas_call(
        functools.partial(down_kernel, dense_rows),
        out_shape=(jax.ShapeDtypeStruct(shape, F32), jax.ShapeDtypeStruct(shape, BF16)),
        grid_spec=pltpu.PrefetchScalarGridSpec(
            num_scalar_prefetch=1,
            grid=(SIDE,),
            in_specs=[pl.BlockSpec((units, rows), lambda i, place: (0, 0))]
            + [weight(False)] * 2
            + [weight(True)] * 2,
            out_specs=(out, out),
        ),
        compiler_params=pltpu.CompilerParams(vmem_limit_bytes=16 * MIB),
        cost_estimate=pl.CostEstimate(
            flops=4 * SIDE * cols * rows * units, bytes_accessed=4 * MIB, transcendentals=0
        ),
        name=f"down_pieces_{outer}",
    )(place, hidden, dense_down, expert_down, dense_down, expert_down)


def shards(
    tokens,
    norm_gain,
    route_ids,
    route_probs,
    dense_gate,
    dense_up,
    dense_down,
    expert_gate,
    expert_up,
    expert_down,
):
    experts = lax.axis_size("expert")
    rows, choose = route_ids.shape
    cols = tokens.shape[1]
    capacity = 3 * rows * choose // (2 * experts)
    index = lax.axis_index("tensor")
    place = jnp.stack([index // (SIDE * PAIR), index // PAIR % SIDE, index % PAIR]).astype(jnp.int32)

    outgoing, combine = dispatched(route_ids.T, route_probs.T, tokens.T, experts, capacity)
    received = lax.all_to_all(
        outgoing.reshape(experts, capacity, cols), "expert", 0, 0, tiled=True
    ).reshape(experts * capacity, cols)
    own = jnp.concatenate([tokens.T, received.T], axis=1)

    first = [own] + [lax.ppermute(own, "tensor", hops(d, True)) for d in range(1, SIDE)]
    stack = jnp.stack(first)
    near, far, left = [lax.ppermute(stack, "tensor", hops(d, False)) for d in (1, 2, 3)]
    stack_other = sibling(stack)
    dense, routed, dense_down, routed_down = piece_weights(
        norm_gain[None, :],
        dense_gate,
        dense_up,
        expert_gate[0],
        expert_up[0],
        dense_down,
        expert_down[0],
        cols,
    )
    add = functools.partial(arrive, place, dense=dense, routed=routed, dense_rows=rows)
    sums = add([(stack, 0, False)], sums=None)
    near, stack_other, sums, dense_down, routed_down = lax.optimization_barrier(
        (near, stack_other, sums, dense_down, routed_down)
    )
    near_other = sibling(near)
    sums = add([(stack_other, 0, True), (near, 1, False)], sums=sums)
    far, left, sums = lax.optimization_barrier((far, left, sums))
    far_other, left_other = sibling(far), sibling(left)
    sums = add([(near_other, 1, True), (far, 2, False), (left, 3, False)], sums=sums)
    far_other, left_other, sums = lax.optimization_barrier((far_other, left_other, sums))
    hidden = add([(far_other, 2, True), (left_other, 3, True)], sums=sums, last=True)

    pieces = {}
    for outer in (1, 2, 3, 0):
        mine, others = down_pieces(place, hidden, dense_down, routed_down, outer, rows)
        if outer > 1:
            pieces[outer - 1], hidden = lax.optimization_barrier((pieces[outer - 1], hidden))
        pieces[outer] = mine + sibling(others).astype(F32)
    level = pieces[0]
    level = pieces[0]
    for d in range(1, SIDE):
        level = level + lax.ppermute(pieces[d].astype(BF16), "tensor", hops(d, False)).astype(F32)
    total = level[0]
    for d in range(1, SIDE):
        total = total + lax.ppermute(level[d].astype(BF16), "tensor", hops(d, True)).astype(F32)

    back = total[:, rows:].astype(BF16).T.reshape(experts, capacity, cols)
    returned = lax.all_to_all(back, "expert", 0, 0, tiled=True).reshape(experts * capacity, cols)
    moe_out = jnp.dot(combine.T, returned.astype(F32), precision=lax.Precision.HIGHEST)
    return (total[:, :rows].T + moe_out).astype(BF16)


def solution(mesh):
    in_specs = (
        P("expert", "tensor"),
        P(),
        P("expert", None),
        P("expert", None),
        P("tensor", None),
        P("tensor", None),
        P("tensor", None),
        P("expert", "tensor", None),
        P("expert", "tensor", None),
        P("expert", "tensor", None),
    )
    out_specs = P("expert", "tensor")
    return jax.shard_map(shards, mesh=mesh, in_specs=in_specs, out_specs=out_specs, check_vma=False)
```

```python
import functools

import jax
import jax.numpy as jnp
from jax import lax
from jax.experimental import pallas as pl
from jax.experimental.pallas import tpu as pltpu
from jax.sharding import PartitionSpec as P

SIDE = 4
PAIR = 2
CHIPS = SIDE * SIDE
GROUP = CHIPS * PAIR
F32 = jnp.float32
BF16 = jnp.bfloat16
MIB = 1024 * 1024
CHUNK = 896


def device_of(x, y, core):
    return (x * SIDE + y) * PAIR + core


def hops(step, first):
    pairs = []
    for x in range(SIDE):
        for y in range(SIDE):
            for core in range(PAIR):
                along_x = (core == 0) == first
                to_x = (x + step) % SIDE if along_x else x
                to_y = y if along_x else (y + step) % SIDE
                pairs.append((device_of(x, y, core), device_of(to_x, to_y, core)))
    return pairs


def sibling(value):
    return lax.ppermute(value, "tensor", [(i, i ^ 1) for i in range(GROUP)])


def piece_index(place, other, sign, outer, inner):
    x, y, core = place[0], place[1], place[2]
    owner = 1 - core if other else core
    move_x = jnp.where(owner == 0, inner, outer)
    move_y = jnp.where(owner == 0, outer, inner)
    at_x = lax.rem(x + sign * move_x + SIDE, SIDE)
    at_y = lax.rem(y + sign * move_y + SIDE, SIDE)
    return device_of(at_x, at_y, owner)


def dispatch_kernel(experts, capacity, ids, probs, tokens, outgoing, combine):
    choose, rows = ids.shape
    slots = experts * capacity
    numbers = lax.broadcasted_iota(jnp.int32, (experts, rows), 0)
    before = lax.broadcasted_iota(jnp.int32, (rows, rows), 0)
    after = lax.broadcasted_iota(jnp.int32, (rows, rows), 1)
    earlier = (before < after).astype(F32).astype(BF16)
    slot_numbers = lax.broadcasted_iota(jnp.int32, (slots, rows), 0)
    taken = jnp.zeros((experts, 1), F32)
    weights = jnp.zeros((slots, rows), F32)
    chosen = jnp.zeros((slots, rows), F32)
    for k in range(choose):
        named = ids[k : k + 1, :]
        onehot = (numbers == named).astype(F32)
        ahead = jnp.dot(onehot.astype(BF16), earlier, preferred_element_type=F32) + taken
        position = jnp.sum(ahead * onehot, axis=0, keepdims=True).astype(jnp.int32)
        hits = slot_numbers == named * capacity + position
        weights = weights + jnp.where(hits, probs[k : k + 1, :], 0.0)
        chosen = chosen + hits.astype(F32)
        taken = taken + jnp.sum(onehot, axis=1, keepdims=True)
    combine[...] = weights
    outgoing[...] = lax.dot_general(
        chosen.astype(BF16), tokens[...], (((1,), (1,)), ((), ())), preferred_element_type=F32
    ).astype(BF16)


def dispatched(ids, probs, tokens, experts, capacity):
    cols, rows = tokens.shape
    return pl.pallas_call(
        functools.partial(dispatch_kernel, experts, capacity),
        out_shape=(
            jax.ShapeDtypeStruct((experts * capacity, cols), BF16),
            jax.ShapeDtypeStruct((experts * capacity, rows), F32),
        ),
        name="dispatch",
    )(ids, probs, tokens)


def fetches(sources, targets, arrived):
    steps = sources[0].shape[1] // CHUNK
    copies = []
    for step in range(steps):
        at = slice(step * CHUNK, (step + 1) * CHUNK)
        copies.append(
            [
                pltpu.make_async_copy(source.at[:, at], target.at[:, at], arrived.at[i, step])
                for i, (source, target) in enumerate(zip(sources, targets))
            ]
        )
    for row in copies:
        for copy in row:
            copy.start()
    return copies


def fetched(count, units, width):
    return [pltpu.VMEM((units, width), BF16)] * count + [
        pltpu.SemaphoreType.DMA((count, width // CHUNK))
    ]


IN_HBM = pl.BlockSpec(memory_space=pltpu.MemorySpace.HBM)
IN_VMEM = pl.BlockSpec(memory_space=pltpu.MemorySpace.VMEM)


def up_weights_kernel(cols, gain, gate_source, up_source, out, gate, up, arrived):
    each = CHUNK // cols
    for step, copies in enumerate(fetches([gate_source, up_source], [gate, up], arrived)):
        for copy in copies:
            copy.wait()
        for i in range(step * each, (step + 1) * each):
            at = slice(i * cols, (i + 1) * cols)
            both = jnp.concatenate([gate[:, at].astype(F32), up[:, at].astype(F32)], axis=0)
            out[i] = (both * gain[:, at]).astype(BF16)


def up_weights(gain, gate, up, cols):
    units, width = gate.shape
    return pl.pallas_call(
        functools.partial(up_weights_kernel, cols),
        out_shape=jax.ShapeDtypeStruct((width // cols, 2 * units, cols), BF16),
        in_specs=[IN_VMEM, IN_HBM, IN_HBM],
        out_specs=IN_VMEM,
        scratch_shapes=fetched(2, units, width),
        compiler_params=pltpu.CompilerParams(vmem_limit_bytes=18 * MIB),
        cost_estimate=pl.CostEstimate(flops=MIB, bytes_accessed=MIB, transcendentals=0),
        name="up_weights",
    )(gain, gate, up)


def down_weights_kernel(cols, first_source, second_source, *refs):
    outs, scratch, arrived = refs[:2], refs[2:4], refs[4]
    each = CHUNK // cols
    for step, copies in enumerate(fetches([first_source, second_source], scratch, arrived)):
        for copy, weight, out in zip(copies, scratch, outs):
            copy.wait()
            for i in range(step * each, (step + 1) * each):
                out[i] = weight[:, i * cols : (i + 1) * cols].astype(F32).T.astype(BF16)


def down_weights(first, second, cols):
    units, width = first.shape
    shape = jax.ShapeDtypeStruct((width // cols, cols, units), BF16)
    return pl.pallas_call(
        functools.partial(down_weights_kernel, cols),
        out_shape=[shape, shape],
        in_specs=[IN_HBM, IN_HBM],
        out_specs=[IN_VMEM, IN_VMEM],
        scratch_shapes=fetched(2, units, width),
        compiler_params=pltpu.CompilerParams(vmem_limit_bytes=20 * MIB),
        cost_estimate=pl.CostEstimate(flops=MIB, bytes_accessed=MIB, transcendentals=0),
        name="down_weights",
    )(first, second)


def dense_kernel(gain, source, gate_source, up_source, hidden, gathered, gate, up, came, arrived):
    width, rows = gathered.shape
    rows_copy = pltpu.make_async_copy(source, gathered, came)
    rows_copy.start()
    copies = fetches([gate_source, up_source], [gate, up], arrived)
    rows_copy.wait()

    def squares(i, total):
        block = gathered[pl.ds(pl.multiple_of(i * CHUNK, CHUNK), CHUNK), :].astype(F32)
        block = block * block
        return total + jnp.sum(block.reshape(CHUNK // 8, 8, rows), axis=0)

    total = lax.fori_loop(0, width // CHUNK, squares, jnp.zeros((8, rows), F32))
    scale = lax.rsqrt(jnp.sum(total, axis=0, keepdims=True) / width + 1e-05)

    def product(weight, normed):
        return lax.dot_general(
            weight, normed, (((1,), (1,)), ((), ())), preferred_element_type=F32
        )

    gates = ups = jnp.zeros((gate.shape[0], rows), F32)
    for step, row in enumerate(copies):
        at = slice(step * CHUNK, (step + 1) * CHUNK)
        normed = ((gathered[at, :].astype(F32) * scale).T * gain[:, at]).astype(BF16)
        for copy in row:
            copy.wait()
        gates = gates + product(gate[:, at], normed)
        ups = ups + product(up[:, at], normed)
    hidden[...] = (gates / (1.0 + jnp.exp(-gates)) * ups).astype(BF16)


def dense_hidden_units(gathered, gain, gate, up):
    units, width = gate.shape
    rows = gathered.shape[1]
    return pl.pallas_call(
        dense_kernel,
        out_shape=jax.ShapeDtypeStruct((units, rows), BF16),
        in_specs=[IN_VMEM, IN_HBM, IN_HBM, IN_HBM],
        out_specs=IN_VMEM,
        scratch_shapes=[
            pltpu.VMEM((width, rows), BF16),
            pltpu.VMEM((units, width), BF16),
            pltpu.VMEM((units, width), BF16),
            pltpu.SemaphoreType.DMA,
            pltpu.SemaphoreType.DMA((2, width // CHUNK)),
        ],
        compiler_params=pltpu.CompilerParams(vmem_limit_bytes=14 * MIB),
        cost_estimate=pl.CostEstimate(flops=MIB, bytes_accessed=MIB, transcendentals=0),
        name="dense_hidden",
    )(gain, gathered, gate, up)


def arrive_kernel(count, start, last, width, place, *refs):
    stacks, weights, refs = refs[:count], refs[count : 2 * count], refs[2 * count :]
    if not start:
        carried, refs = refs[:2], refs[2:]
    if last:
        hidden, refs = refs[0], refs[1:]
    sums, squares = refs

    @pl.when(pl.program_id(0) == 0)
    def _():
        for i, ref in enumerate((sums, squares)):
            ref[...] = jnp.zeros_like(ref) if start else carried[i][...]

    for stack, weight in zip(stacks, weights):
        block = stack[0]
        sums[...] += jnp.dot(weight[0], block, preferred_element_type=F32)
        values = block.astype(F32)
        values = values * values
        squares[...] += jnp.sum(values.reshape(values.shape[0] // 8, 8, values.shape[1]), axis=0)

    if last:

        @pl.when(pl.program_id(0) == pl.num_programs(0) - 1)
        def _():
            scale = lax.rsqrt(jnp.sum(squares[...], axis=0, keepdims=True) / width + 1e-05)
            units = sums.shape[0] // 2
            gates, ups = sums[:units, :] * scale, sums[units:, :] * scale
            hidden[...] = (gates / (1.0 + jnp.exp(-gates)) * ups).astype(BF16)


def arrive(place, stage, weights, sums, last=False):
    count = len(stage)
    cols, rows = stage[0][0].shape[1:]
    height = weights.shape[1]
    start = sums is None

    def weight(outer, other):
        def index(i, place):
            return piece_index(place, other, -1, outer, i), 0, 0

        return pl.BlockSpec((1, height, cols), index)

    whole = lambda shape: pl.BlockSpec(shape, lambda i, place: (0, 0))
    shapes = [(height, rows), (8, rows)]
    sum_specs = [whole(s) for s in shapes]
    if last:
        out_specs = whole((height // 2, rows))
        out_shape = jax.ShapeDtypeStruct((height // 2, rows), BF16)
        scratch = [pltpu.VMEM(s, F32) for s in shapes]
    else:
        out_specs, scratch = sum_specs, []
        out_shape = [jax.ShapeDtypeStruct(s, F32) for s in shapes]
    return pl.pallas_call(
        functools.partial(arrive_kernel, count, start, last, GROUP * cols),
        out_shape=out_shape,
        grid_spec=pltpu.PrefetchScalarGridSpec(
            num_scalar_prefetch=1,
            grid=(SIDE,),
            in_specs=[pl.BlockSpec((1, cols, rows), lambda i, place: (i, 0, 0))] * count
            + [weight(outer, other) for _, outer, other in stage]
            + ([] if start else sum_specs),
            out_specs=out_specs,
            scratch_shapes=scratch,
        ),
        compiler_params=pltpu.CompilerParams(vmem_limit_bytes=8 * MIB),
        cost_estimate=pl.CostEstimate(flops=MIB, bytes_accessed=MIB, transcendentals=0),
        name=f"arrive_{stage[-1][1]}_{count}",
    )(
        place,
        *[stack for stack, _, _ in stage],
        *[weights] * count,
        *([] if start else sums),
    )


def down_kernel(place, hidden, weight, other_weight, mine, others):
    mine[0] = jnp.dot(weight[0], hidden[...], preferred_element_type=F32)
    others[0] = jnp.dot(other_weight[0], hidden[...], preferred_element_type=F32).astype(BF16)


def down_pieces(place, hidden, weights, first, steps):
    units, rows = hidden.shape
    cols = weights.shape[1]

    def weight(other):
        def index(i, place):
            return piece_index(place, other, 1, first + i // SIDE, i % SIDE), 0, 0

        return pl.BlockSpec((1, cols, units), index)

    out = pl.BlockSpec((1, cols, rows), lambda i, place: (i, 0, 0))
    shape = (steps * SIDE, cols, rows)
    return pl.pallas_call(
        down_kernel,
        out_shape=(jax.ShapeDtypeStruct(shape, F32), jax.ShapeDtypeStruct(shape, BF16)),
        grid_spec=pltpu.PrefetchScalarGridSpec(
            num_scalar_prefetch=1,
            grid=(steps * SIDE,),
            in_specs=[
                pl.BlockSpec((units, rows), lambda i, place: (0, 0)),
                weight(False),
                weight(True),
            ],
            out_specs=(out, out),
        ),
        compiler_params=pltpu.CompilerParams(vmem_limit_bytes=8 * MIB),
        cost_estimate=pl.CostEstimate(flops=MIB, bytes_accessed=MIB, transcendentals=0),
        name=f"down_pieces_{first}_{steps}",
    )(place, hidden, weights, weights)


def shards(
    tokens,
    norm_gain,
    route_ids,
    route_probs,
    dense_gate,
    dense_up,
    dense_down,
    expert_gate,
    expert_up,
    expert_down,
):
    experts = lax.axis_size("expert")
    rows, choose = route_ids.shape
    cols = tokens.shape[1]
    capacity = 3 * rows * choose // (2 * experts)
    index = lax.axis_index("tensor")
    place = jnp.stack([index // (SIDE * PAIR), index // PAIR % SIDE, index % PAIR]).astype(jnp.int32)

    gain = norm_gain[None, :]

    gathered = lax.all_gather(tokens.T, "tensor", axis=0, tiled=True)

    outgoing, combine = dispatched(route_ids.T, route_probs.T, tokens.T, experts, capacity)
    received = lax.all_to_all(
        outgoing.reshape(experts, capacity, cols), "expert", 0, 0, tiled=True
    ).reshape(experts * capacity, cols)
    own = received.T

    first = [own] + [lax.ppermute(own, "tensor", hops(d, True)) for d in range(1, SIDE)]
    stack = jnp.stack(first)
    near, far, left = [lax.ppermute(stack, "tensor", hops(d, False)) for d in (1, 2, 3)]
    stack_other = sibling(stack)
    weights = up_weights(gain, expert_gate[0], expert_up[0], cols)
    sums = arrive(place, [(stack, 0, False)], weights, None)
    near, stack_other, sums, expert_down = lax.optimization_barrier(
        (near, stack_other, sums, expert_down)
    )
    near_other = sibling(near)
    sums = arrive(place, [(stack_other, 0, True), (near, 1, False)], weights, sums)
    routed_down, dense_down = down_weights(expert_down[0], dense_down, cols)
    far, left, sums, routed_down, dense_down = lax.optimization_barrier(
        (far, left, sums, routed_down, dense_down)
    )
    far_other, left_other = sibling(far), sibling(left)
    sums = arrive(
        place, [(near_other, 1, True), (far, 2, False), (left, 3, False)], weights, sums
    )
    far_other, left_other, sums = lax.optimization_barrier((far_other, left_other, sums))
    hidden = arrive(
        place, [(far_other, 2, True), (left_other, 3, True)], weights, sums, last=True
    )

    hidden, gathered = lax.optimization_barrier((hidden, gathered))

    pieces = {}
    for outer in (1, 2, 3, 0):
        mine, others = down_pieces(place, hidden, routed_down, outer, 1)
        if outer > 1:
            pieces[outer - 1], hidden = lax.optimization_barrier((pieces[outer - 1], hidden))
        pieces[outer] = mine + sibling(others).astype(F32)
    leaving = [pieces[d].astype(BF16) for d in range(1, SIDE)]

    summed = [lax.ppermute(part, "tensor", hops(d, False)) for d, part in zip((1, 2, 3), leaving)]

    gathered, summed[0] = lax.optimization_barrier((gathered, summed[0]))
    dense_hidden = dense_hidden_units(gathered, gain, dense_gate, dense_up)
    mine, others = down_pieces(place, dense_hidden, dense_down, 0, SIDE)
    dense_pieces = (mine + sibling(others).astype(F32)).reshape(SIDE, SIDE, cols, rows)

    level = pieces[0]
    for part in summed:
        level = level + part.astype(F32)
    total = level[0]
    for d in range(1, SIDE):
        total = total + lax.ppermute(level[d].astype(BF16), "tensor", hops(d, True)).astype(F32)

    dense_level = dense_pieces[0]
    for d in range(1, SIDE):
        dense_level = dense_level + lax.ppermute(
            dense_pieces[d].astype(BF16), "tensor", hops(d, False)
        ).astype(F32)
    dense_total = dense_level[0]
    for d in range(1, SIDE):
        dense_total = dense_total + lax.ppermute(
            dense_level[d].astype(BF16), "tensor", hops(d, True)
        ).astype(F32)

    back = total.astype(BF16).T.reshape(experts, capacity, cols)
    returned = lax.all_to_all(back, "expert", 0, 0, tiled=True).reshape(experts * capacity, cols)
    moe_out = jnp.dot(combine.T, returned.astype(F32), precision=lax.Precision.HIGHEST)
    return (dense_total.T + moe_out).astype(BF16)


def solution(mesh):
    in_specs = (
        P("expert", "tensor"),
        P(),
        P("expert", None),
        P("expert", None),
        P("tensor", None),
        P("tensor", None),
        P("tensor", None),
        P("expert", "tensor", None),
        P("expert", "tensor", None),
        P("expert", "tensor", None),
    )
    out_specs = P("expert", "tensor")
    return jax.shard_map(shards, mesh=mesh, in_specs=in_specs, out_specs=out_specs, check_vma=False)
```

```python
import functools

import jax
import jax.numpy as jnp
from jax import lax
from jax.experimental import pallas as pl
from jax.experimental.pallas import tpu as pltpu
from jax.sharding import PartitionSpec as P

SIDE = 4
PAIR = 2
CHIPS = SIDE * SIDE
GROUP = CHIPS * PAIR
F32 = jnp.float32
BF16 = jnp.bfloat16
MIB = 1024 * 1024
CHUNK = 896


def device_of(x, y, core):
    return (x * SIDE + y) * PAIR + core


def hops(step, first):
    pairs = []
    for x in range(SIDE):
        for y in range(SIDE):
            for core in range(PAIR):
                along_x = (core == 0) == first
                to_x = (x + step) % SIDE if along_x else x
                to_y = y if along_x else (y + step) % SIDE
                pairs.append((device_of(x, y, core), device_of(to_x, to_y, core)))
    return pairs


def sibling(value):
    return lax.ppermute(value, "tensor", [(i, i ^ 1) for i in range(GROUP)])


def piece_index(place, other, sign, outer, inner):
    x, y, core = place[0], place[1], place[2]
    owner = 1 - core if other else core
    move_x = jnp.where(owner == 0, inner, outer)
    move_y = jnp.where(owner == 0, outer, inner)
    at_x = lax.rem(x + sign * move_x + SIDE, SIDE)
    at_y = lax.rem(y + sign * move_y + SIDE, SIDE)
    return device_of(at_x, at_y, owner)


def dispatch_kernel(experts, capacity, ids, probs, tokens, outgoing, combine):
    choose, rows = ids.shape
    slots = experts * capacity
    numbers = lax.broadcasted_iota(jnp.int32, (experts, rows), 0)
    before = lax.broadcasted_iota(jnp.int32, (rows, rows), 0)
    after = lax.broadcasted_iota(jnp.int32, (rows, rows), 1)
    earlier = (before < after).astype(F32).astype(BF16)
    slot_numbers = lax.broadcasted_iota(jnp.int32, (slots, rows), 0)
    taken = jnp.zeros((experts, 1), F32)
    weights = jnp.zeros((slots, rows), F32)
    chosen = jnp.zeros((slots, rows), F32)
    for k in range(choose):
        named = ids[k : k + 1, :]
        onehot = (numbers == named).astype(F32)
        ahead = jnp.dot(onehot.astype(BF16), earlier, preferred_element_type=F32) + taken
        position = jnp.sum(ahead * onehot, axis=0, keepdims=True).astype(jnp.int32)
        hits = slot_numbers == named * capacity + position
        weights = weights + jnp.where(hits, probs[k : k + 1, :], 0.0)
        chosen = chosen + hits.astype(F32)
        taken = taken + jnp.sum(onehot, axis=1, keepdims=True)
    combine[...] = weights
    outgoing[...] = lax.dot_general(
        chosen.astype(BF16), tokens[...], (((1,), (1,)), ((), ())), preferred_element_type=F32
    ).astype(BF16)


def dispatched(ids, probs, tokens, experts, capacity):
    cols, rows = tokens.shape
    return pl.pallas_call(
        functools.partial(dispatch_kernel, experts, capacity),
        out_shape=(
            jax.ShapeDtypeStruct((experts * capacity, cols), BF16),
            jax.ShapeDtypeStruct((experts * capacity, rows), F32),
        ),
        name="dispatch",
    )(ids, probs, tokens)


def fetches(sources, targets, arrived):
    steps = sources[0].shape[1] // CHUNK
    copies = []
    for step in range(steps):
        at = slice(step * CHUNK, (step + 1) * CHUNK)
        copies.append(
            [
                pltpu.make_async_copy(source.at[:, at], target.at[:, at], arrived.at[i, step])
                for i, (source, target) in enumerate(zip(sources, targets))
            ]
        )
    for row in copies:
        for copy in row:
            copy.start()
    return copies


def fetched(count, units, width):
    return [pltpu.VMEM((units, width), BF16)] * count + [
        pltpu.SemaphoreType.DMA((count, width // CHUNK))
    ]


IN_HBM = pl.BlockSpec(memory_space=pltpu.MemorySpace.HBM)
IN_VMEM = pl.BlockSpec(memory_space=pltpu.MemorySpace.VMEM)


def up_weights_kernel(cols, gain, gate_source, up_source, out, gate, up, arrived):
    each = CHUNK // cols
    for step, copies in enumerate(fetches([gate_source, up_source], [gate, up], arrived)):
        for copy in copies:
            copy.wait()
        for i in range(step * each, (step + 1) * each):
            at = slice(i * cols, (i + 1) * cols)
            both = jnp.concatenate([gate[:, at].astype(F32), up[:, at].astype(F32)], axis=0)
            out[i] = (both * gain[:, at]).astype(BF16)


def up_weights(gain, gate, up, cols):
    units, width = gate.shape
    return pl.pallas_call(
        functools.partial(up_weights_kernel, cols),
        out_shape=jax.ShapeDtypeStruct((width // cols, 2 * units, cols), BF16),
        in_specs=[IN_VMEM, IN_HBM, IN_HBM],
        out_specs=IN_VMEM,
        scratch_shapes=fetched(2, units, width),
        compiler_params=pltpu.CompilerParams(vmem_limit_bytes=18 * MIB),
        cost_estimate=pl.CostEstimate(flops=MIB, bytes_accessed=MIB, transcendentals=0),
        name="up_weights",
    )(gain, gate, up)


def down_weights_kernel(cols, source, out, weight, arrived):
    each = CHUNK // cols
    for step, (copy,) in enumerate(fetches([source], [weight], arrived)):
        copy.wait()
        for i in range(step * each, (step + 1) * each):
            out[i] = weight[:, i * cols : (i + 1) * cols].astype(F32).T.astype(BF16)


def down_weights(down, cols):
    units, width = down.shape
    return pl.pallas_call(
        functools.partial(down_weights_kernel, cols),
        out_shape=jax.ShapeDtypeStruct((width // cols, cols, units), BF16),
        in_specs=[IN_HBM],
        out_specs=IN_VMEM,
        scratch_shapes=fetched(1, units, width),
        compiler_params=pltpu.CompilerParams(vmem_limit_bytes=12 * MIB),
        cost_estimate=pl.CostEstimate(flops=MIB, bytes_accessed=MIB, transcendentals=0),
        name="down_weights",
    )(down)


def arrive_kernel(dense_rows, count, start, last, width, place, *refs):
    stacks, dense, routed = (refs[i * count : (i + 1) * count] for i in range(3))
    refs = refs[3 * count :]
    if not start:
        carried, refs = refs[:3], refs[3:]
    if last:
        hidden, refs = refs[0], refs[1:]
    dense_sum, routed_sum, squares = refs

    @pl.when(pl.program_id(0) == 0)
    def _():
        for i, ref in enumerate(refs):
            ref[...] = jnp.zeros_like(ref) if start else carried[i][...]

    for stack, dense_weight, routed_weight in zip(stacks, dense, routed):
        block = stack[0]
        dense_sum[...] += jnp.dot(
            dense_weight[0], block[:, :dense_rows], preferred_element_type=F32
        )
        routed_sum[...] += jnp.dot(
            routed_weight[0], block[:, dense_rows:], preferred_element_type=F32
        )
        values = block.astype(F32)
        values = values * values
        squares[...] += jnp.sum(values.reshape(values.shape[0] // 8, 8, values.shape[1]), axis=0)

    if last:

        @pl.when(pl.program_id(0) == pl.num_programs(0) - 1)
        def _():
            scale = lax.rsqrt(jnp.sum(squares[...], axis=0, keepdims=True) / width + 1e-05)
            units = dense_sum.shape[0] // 2
            for sums, span in (
                (dense_sum, slice(0, dense_rows)),
                (routed_sum, slice(dense_rows, scale.shape[1])),
            ):
                gates = sums[:units, :] * scale[:, span]
                ups = sums[units:, :] * scale[:, span]
                hidden[:, span] = (gates / (1.0 + jnp.exp(-gates)) * ups).astype(BF16)


def arrive(place, stage, weights, sums, dense_rows, last=False):
    count = len(stage)
    pieces, cols, rows = stage[0][0].shape
    height = weights[0].shape[1]
    start = sums is None

    def weight(outer, inner, other):
        def index(i, place):
            return piece_index(place, other, -1, outer, inner + i), 0, 0

        return pl.BlockSpec((1, height, cols), index)

    whole = lambda shape: pl.BlockSpec(shape, lambda i, place: (0, 0))
    shapes = [(height, dense_rows), (height, rows - dense_rows), (8, rows)]
    sum_specs = [whole(s) for s in shapes]
    if last:
        out_specs = whole((height // 2, rows))
        out_shape = jax.ShapeDtypeStruct((height // 2, rows), BF16)
        scratch = [pltpu.VMEM(s, F32) for s in shapes]
    else:
        out_specs, scratch = sum_specs, []
        out_shape = [jax.ShapeDtypeStruct(s, F32) for s in shapes]
    return pl.pallas_call(
        functools.partial(arrive_kernel, dense_rows, count, start, last, GROUP * cols),
        out_shape=out_shape,
        grid_spec=pltpu.PrefetchScalarGridSpec(
            num_scalar_prefetch=1,
            grid=(pieces,),
            in_specs=[pl.BlockSpec((1, cols, rows), lambda i, place: (i, 0, 0))] * count
            + [weight(*rest) for _, *rest in stage] * 2
            + ([] if start else sum_specs),
            out_specs=out_specs,
            scratch_shapes=scratch,
        ),
        compiler_params=pltpu.CompilerParams(vmem_limit_bytes=12 * MIB),
        cost_estimate=pl.CostEstimate(flops=MIB, bytes_accessed=MIB, transcendentals=0),
        name=f"arrive_{stage[-1][1]}_{count}",
    )(
        place,
        *[stack for stack, *_ in stage],
        *[weights[0]] * count,
        *[weights[1]] * count,
        *([] if start else sums),
    )


def down_kernel(dense_rows, place, hidden, *refs):
    mine, others = refs[4:]
    for out, dense, routed in ((mine, refs[0], refs[1]), (others, refs[2], refs[3])):
        for weight, span in (
            (dense, slice(0, dense_rows)),
            (routed, slice(dense_rows, hidden.shape[1])),
        ):
            out[0, :, span] = jnp.dot(
                weight[0], hidden[:, span], preferred_element_type=F32
            ).astype(out.dtype)


def down_pieces(place, hidden, weights, outer, dense_rows):
    units, rows = hidden.shape
    cols = weights[0].shape[1]

    def weight(other):
        def index(i, place):
            return piece_index(place, other, 1, outer, i), 0, 0

        return pl.BlockSpec((1, cols, units), index)

    out = pl.BlockSpec((1, cols, rows), lambda i, place: (i, 0, 0))
    shape = (SIDE, cols, rows)
    return pl.pallas_call(
        functools.partial(down_kernel, dense_rows),
        out_shape=(jax.ShapeDtypeStruct(shape, F32), jax.ShapeDtypeStruct(shape, BF16)),
        grid_spec=pltpu.PrefetchScalarGridSpec(
            num_scalar_prefetch=1,
            grid=(SIDE,),
            in_specs=[pl.BlockSpec((units, rows), lambda i, place: (0, 0))]
            + [weight(False)] * 2
            + [weight(True)] * 2,
            out_specs=(out, out),
        ),
        compiler_params=pltpu.CompilerParams(vmem_limit_bytes=8 * MIB),
        cost_estimate=pl.CostEstimate(flops=MIB, bytes_accessed=MIB, transcendentals=0),
        name=f"down_pieces_{outer}",
    )(place, hidden, weights[0], weights[1], weights[0], weights[1])


def shards(
    tokens,
    norm_gain,
    route_ids,
    route_probs,
    dense_gate,
    dense_up,
    dense_down,
    expert_gate,
    expert_up,
    expert_down,
):
    experts = lax.axis_size("expert")
    rows, choose = route_ids.shape
    cols = tokens.shape[1]
    capacity = 3 * rows * choose // (2 * experts)
    index = lax.axis_index("tensor")
    place = jnp.stack([index // (SIDE * PAIR), index // PAIR % SIDE, index % PAIR]).astype(jnp.int32)

    gain = norm_gain[None, :]

    outgoing, combine = dispatched(route_ids.T, route_probs.T, tokens.T, experts, capacity)
    received = lax.all_to_all(
        outgoing.reshape(experts, capacity, cols), "expert", 0, 0, tiled=True
    ).reshape(experts * capacity, cols)
    weights = [
        up_weights(gain, dense_gate, dense_up, cols),
        up_weights(gain, expert_gate[0], expert_up[0], cols),
    ]
    received, weights = lax.optimization_barrier((received, weights))
    own = jnp.concatenate([tokens.T, received.T], axis=1)

    def level_one(value, d):
        return lax.ppermute(value, "tensor", hops(d, True))

    def level_two(value, d):
        return lax.ppermute(value, "tensor", hops(d, False))

    half = SIDE // 2
    arrived = [level_one(own, d) for d in range(1, SIDE)]
    routed_down = down_weights(expert_down[0], cols)
    arrived, routed_down = lax.optimization_barrier((arrived, routed_down))
    stack = jnp.stack([own] + arrived)
    low, high = stack[:half], stack[half:]
    back_low, on_high = level_two(low, 1), level_two(high, 3)
    back_high, on_low = level_two(high, 1), level_two(low, 3)
    stack_other = sibling(stack)
    add = functools.partial(arrive, place, weights=weights, dense_rows=rows)
    sums = add([(stack, 0, 0, False)], sums=None)
    down = [down_weights(dense_down, cols), routed_down]
    back_low, on_high, sums, down = lax.optimization_barrier((back_low, on_high, sums, down))
    far_low, far_high = level_two(back_low, 1), level_two(on_high, 3)
    sums = add([(stack_other, 0, 0, True)], sums=sums)
    near = [(back_low, 1, 0), (on_high, 3, half), (back_high, 1, half), (on_low, 3, 0)]
    sums = add([(part, outer, inner, False) for part, outer, inner in near[:2]], sums=sums)
    others = [(sibling(part), outer, inner, True) for part, outer, inner in near]
    sums = add([(part, outer, inner, False) for part, outer, inner in near[2:]], sums=sums)
    far_low, far_high, sums = lax.optimization_barrier((far_low, far_high, sums))
    far = [(far_low, 2, 0), (far_high, 2, half)]
    far_others = [(sibling(part), outer, inner, True) for part, outer, inner in far]
    sums = add(others + [(part, outer, inner, False) for part, outer, inner in far], sums=sums)
    hidden = add(far_others, sums=sums, last=True)

    def both_cores(outer, hidden):
        mine, others = down_pieces(place, hidden, down, outer, rows)
        return mine + sibling(others).astype(F32)

    def sent(value, level, d):
        return level(value.astype(BF16), d).astype(F32)

    pieces = both_cores(2, hidden)
    from_back, from_on = sent(pieces[:half], level_two, 1), sent(pieces[half:], level_two, 3)
    to_on = both_cores(1, hidden)
    on_part = sent(to_on[half:], level_two, 1)
    to_back = both_cores(3, hidden)
    back_part = sent(to_back[:half], level_two, 3)
    staying = both_cores(0, hidden)
    on_sum = sent(to_on[:half] + from_back, level_two, 1)
    back_sum = sent(to_back[half:] + from_on, level_two, 3)
    level = staying + jnp.concatenate([on_sum + back_part, on_part + back_sum])
    total = level[0]
    for d in range(1, SIDE):
        total = total + sent(level[d], level_one, d)

    back = total[:, rows:].astype(BF16).T.reshape(experts, capacity, cols)
    returned = lax.all_to_all(back, "expert", 0, 0, tiled=True).reshape(experts * capacity, cols)
    moe_out = jnp.dot(combine.T, returned.astype(F32), precision=lax.Precision.HIGHEST)
    return (total[:, :rows].T + moe_out).astype(BF16)


def solution(mesh):
    in_specs = (
        P("expert", "tensor"),
        P(),
        P("expert", None),
        P("expert", None),
        P("tensor", None),
        P("tensor", None),
        P("tensor", None),
        P("expert", "tensor", None),
        P("expert", "tensor", None),
        P("expert", "tensor", None),
    )
    out_specs = P("expert", "tensor")
    return jax.shard_map(shards, mesh=mesh, in_specs=in_specs, out_specs=out_specs, check_vma=False)
```

```python
import functools

import jax
import jax.numpy as jnp
from jax import lax
from jax.experimental import pallas as pl
from jax.experimental.pallas import tpu as pltpu
from jax.sharding import PartitionSpec as P

SIDE = 4
PAIR = 2
CHIPS = SIDE * SIDE
GROUP = CHIPS * PAIR
F32 = jnp.float32
BF16 = jnp.bfloat16
MIB = 1024 * 1024
MOST = 56 * MIB
CHUNK = 896
SMALL = pl.CostEstimate(flops=MIB, bytes_accessed=MIB, transcendentals=0)


def device_of(x, y, core):
    return (x * SIDE + y) * PAIR + core


def hops(step, first):
    pairs = []
    for x in range(SIDE):
        for y in range(SIDE):
            for core in range(PAIR):
                along_x = (core == 0) == first
                to_x = (x + step) % SIDE if along_x else x
                to_y = y if along_x else (y + step) % SIDE
                pairs.append((device_of(x, y, core), device_of(to_x, to_y, core)))
    return pairs


def sibling(value):
    return lax.ppermute(value, "tensor", [(i, i ^ 1) for i in range(GROUP)])


def piece_index(place, other, sign, outer, inner):
    x, y, core = place[0], place[1], place[2]
    owner = 1 - core if other else core
    move_x = jnp.where(owner == 0, inner, outer)
    move_y = jnp.where(owner == 0, outer, inner)
    at_x = lax.rem(x + sign * move_x + SIDE, SIDE)
    at_y = lax.rem(y + sign * move_y + SIDE, SIDE)
    return device_of(at_x, at_y, owner)


def dispatch_kernel(experts, capacity, ids, probs, tokens, outgoing, combine):
    choose, rows = ids.shape
    slots = experts * capacity
    numbers = lax.broadcasted_iota(jnp.int32, (experts, rows), 0)
    before = lax.broadcasted_iota(jnp.int32, (rows, rows), 0)
    after = lax.broadcasted_iota(jnp.int32, (rows, rows), 1)
    earlier = (before < after).astype(F32).astype(BF16)
    slot_numbers = lax.broadcasted_iota(jnp.int32, (slots, rows), 0)
    taken = jnp.zeros((experts, 1), F32)
    weights = jnp.zeros((slots, rows), F32)
    chosen = jnp.zeros((slots, rows), F32)
    for k in range(choose):
        named = ids[k : k + 1, :]
        onehot = (numbers == named).astype(F32)
        ahead = jnp.dot(onehot.astype(BF16), earlier, preferred_element_type=F32) + taken
        position = jnp.sum(ahead * onehot, axis=0, keepdims=True).astype(jnp.int32)
        hits = slot_numbers == named * capacity + position
        weights = weights + jnp.where(hits, probs[k : k + 1, :], 0.0)
        chosen = chosen + hits.astype(F32)
        taken = taken + jnp.sum(onehot, axis=1, keepdims=True)
    combine[...] = weights
    outgoing[...] = lax.dot_general(
        chosen.astype(BF16), tokens[...], (((1,), (1,)), ((), ())), preferred_element_type=F32
    ).astype(BF16)


def dispatched(ids, probs, tokens, experts, capacity):
    cols, rows = tokens.shape
    return pl.pallas_call(
        functools.partial(dispatch_kernel, experts, capacity),
        out_shape=(
            jax.ShapeDtypeStruct((experts * capacity, cols), BF16),
            jax.ShapeDtypeStruct((experts * capacity, rows), F32),
        ),
        name="dispatch",
    )(ids, probs, tokens)


def up_weights_kernel(cols, gain, gate, up, out):
    for i in range(gate.shape[1] // cols):
        at = slice(i * cols, (i + 1) * cols)
        both = jnp.concatenate([gate[:, at].astype(F32), up[:, at].astype(F32)], axis=0)
        out[i] = (both * gain[:, at]).astype(BF16)


def up_weights(gain, gate, up, cols):
    units, width = gate.shape
    wide = pl.BlockSpec((units, CHUNK), lambda i: (0, i))
    return pl.pallas_call(
        functools.partial(up_weights_kernel, cols),
        out_shape=jax.ShapeDtypeStruct((width // cols, 2 * units, cols), BF16),
        grid=(width // CHUNK,),
        in_specs=[pl.BlockSpec((1, CHUNK), lambda i: (0, i)), wide, wide],
        out_specs=pl.BlockSpec((CHUNK // cols, 2 * units, cols), lambda i: (i, 0, 0)),
        compiler_params=pltpu.CompilerParams(vmem_limit_bytes=MOST),
        cost_estimate=SMALL,
        name="up_weights",
    )(gain, gate, up)


def down_weights_kernel(cols, down, out):
    for i in range(down.shape[1] // cols):
        out[i] = down[:, i * cols : (i + 1) * cols].astype(F32).T.astype(BF16)


def down_weights(down, cols):
    units, width = down.shape
    return pl.pallas_call(
        functools.partial(down_weights_kernel, cols),
        out_shape=jax.ShapeDtypeStruct((width // cols, cols, units), BF16),
        grid=(width // CHUNK,),
        in_specs=[pl.BlockSpec((units, CHUNK), lambda i: (0, i))],
        out_specs=pl.BlockSpec((CHUNK // cols, cols, units), lambda i: (i, 0, 0)),
        compiler_params=pltpu.CompilerParams(vmem_limit_bytes=MOST),
        cost_estimate=SMALL,
        name="down_weights",
    )(down)


def arrive_kernel(dense_rows, count, start, last, width, place, *refs):
    stacks, dense, routed = (refs[i * count : (i + 1) * count] for i in range(3))
    refs = refs[3 * count :]
    if not start:
        carried, refs = refs[:3], refs[3:]
    if last:
        hidden, refs = refs[0], refs[1:]
    dense_sum, routed_sum, squares = refs

    @pl.when(pl.program_id(0) == 0)
    def _():
        for i, ref in enumerate(refs):
            ref[...] = jnp.zeros_like(ref) if start else carried[i][...]

    for stack, dense_weight, routed_weight in zip(stacks, dense, routed):
        block = stack[0]
        dense_sum[...] += jnp.dot(
            dense_weight[0], block[:, :dense_rows], preferred_element_type=F32
        )
        routed_sum[...] += jnp.dot(
            routed_weight[0], block[:, dense_rows:], preferred_element_type=F32
        )
        values = block.astype(F32)
        values = values * values
        squares[...] += jnp.sum(values.reshape(values.shape[0] // 8, 8, values.shape[1]), axis=0)

    if last:

        @pl.when(pl.program_id(0) == pl.num_programs(0) - 1)
        def _():
            scale = lax.rsqrt(jnp.sum(squares[...], axis=0, keepdims=True) / width + 1e-05)
            units = dense_sum.shape[0] // 2
            for sums, span in (
                (dense_sum, slice(0, dense_rows)),
                (routed_sum, slice(dense_rows, scale.shape[1])),
            ):
                gates = sums[:units, :] * scale[:, span]
                ups = sums[units:, :] * scale[:, span]
                hidden[:, span] = (gates / (1.0 + jnp.exp(-gates)) * ups).astype(BF16)


def arrive(place, stage, weights, sums, dense_rows, last=False):
    count = len(stage)
    pieces, cols, rows = stage[0][0].shape
    height = weights[0].shape[1]
    start = sums is None

    def weight(outer, inner, other):
        def index(i, place):
            return piece_index(place, other, -1, outer, inner + i), 0, 0

        return pl.BlockSpec((1, height, cols), index)

    whole = lambda shape: pl.BlockSpec(shape, lambda i, place: (0, 0))
    shapes = [(height, dense_rows), (height, rows - dense_rows), (8, rows)]
    sum_specs = [whole(s) for s in shapes]
    if last:
        out_specs = whole((height // 2, rows))
        out_shape = jax.ShapeDtypeStruct((height // 2, rows), BF16)
        scratch = [pltpu.VMEM(s, F32) for s in shapes]
    else:
        out_specs, scratch = sum_specs, []
        out_shape = [jax.ShapeDtypeStruct(s, F32) for s in shapes]
    return pl.pallas_call(
        functools.partial(arrive_kernel, dense_rows, count, start, last, GROUP * cols),
        out_shape=out_shape,
        grid_spec=pltpu.PrefetchScalarGridSpec(
            num_scalar_prefetch=1,
            grid=(pieces,),
            in_specs=[pl.BlockSpec((1, cols, rows), lambda i, place: (i, 0, 0))] * count
            + [weight(*rest) for _, *rest in stage] * 2
            + ([] if start else sum_specs),
            out_specs=out_specs,
            scratch_shapes=scratch,
        ),
        compiler_params=pltpu.CompilerParams(vmem_limit_bytes=24 * MIB),
        cost_estimate=SMALL,
        name=f"arrive_{stage[-1][1]}_{count}",
    )(
        place,
        *[stack for stack, *_ in stage],
        *[weights[0]] * count,
        *[weights[1]] * count,
        *([] if start else sums),
    )


def down_kernel(dense_rows, place, hidden, *refs):
    mine, others = refs[4:]
    for out, dense, routed in ((mine, refs[0], refs[1]), (others, refs[2], refs[3])):
        for weight, span in (
            (dense, slice(0, dense_rows)),
            (routed, slice(dense_rows, hidden.shape[1])),
        ):
            out[0, :, span] = jnp.dot(
                weight[0], hidden[:, span], preferred_element_type=F32
            ).astype(out.dtype)


def down_pieces(place, hidden, weights, outer, dense_rows):
    units, rows = hidden.shape
    cols = weights[0].shape[1]

    def weight(other):
        def index(i, place):
            return piece_index(place, other, 1, outer, i), 0, 0

        return pl.BlockSpec((1, cols, units), index)

    out = pl.BlockSpec((1, cols, rows), lambda i, place: (i, 0, 0))
    shape = (SIDE, cols, rows)
    return pl.pallas_call(
        functools.partial(down_kernel, dense_rows),
        out_shape=(jax.ShapeDtypeStruct(shape, F32), jax.ShapeDtypeStruct(shape, BF16)),
        grid_spec=pltpu.PrefetchScalarGridSpec(
            num_scalar_prefetch=1,
            grid=(SIDE,),
            in_specs=[pl.BlockSpec((units, rows), lambda i, place: (0, 0))]
            + [weight(False)] * 2
            + [weight(True)] * 2,
            out_specs=(out, out),
        ),
        compiler_params=pltpu.CompilerParams(vmem_limit_bytes=16 * MIB),
        cost_estimate=SMALL,
        name=f"down_pieces_{outer}",
    )(place, hidden, weights[0], weights[1], weights[0], weights[1])


def shards(
    tokens,
    norm_gain,
    route_ids,
    route_probs,
    dense_gate,
    dense_up,
    dense_down,
    expert_gate,
    expert_up,
    expert_down,
):
    experts = lax.axis_size("expert")
    rows, choose = route_ids.shape
    cols = tokens.shape[1]
    capacity = 3 * rows * choose // (2 * experts)
    index = lax.axis_index("tensor")
    place = jnp.stack([index // (SIDE * PAIR), index // PAIR % SIDE, index % PAIR]).astype(jnp.int32)

    gain = norm_gain[None, :]

    outgoing, combine = dispatched(route_ids.T, route_probs.T, tokens.T, experts, capacity)
    received = lax.all_to_all(
        outgoing.reshape(experts, capacity, cols), "expert", 0, 0, tiled=True
    ).reshape(experts * capacity, cols)
    weights = [
        up_weights(gain, dense_gate, dense_up, cols),
        up_weights(gain, expert_gate[0], expert_up[0], cols),
    ]
    received, weights = lax.optimization_barrier((received, weights))
    own = jnp.concatenate([tokens.T, received.T], axis=1)

    def level_one(value, d):
        return lax.ppermute(value, "tensor", hops(d, True))

    def level_two(value, d):
        return lax.ppermute(value, "tensor", hops(d, False))

    arrived = [level_one(own, d) for d in range(1, SIDE)]
    routed_down = down_weights(expert_down[0], cols)
    arrived, routed_down = lax.optimization_barrier((arrived, routed_down))
    stack = jnp.stack([own] + arrived)
    near, far, left = [level_two(stack, d) for d in range(1, SIDE)]
    stack_other = sibling(stack)
    down = [down_weights(dense_down, cols), routed_down]
    add = functools.partial(arrive, place, weights=weights, dense_rows=rows)
    sums = add([(stack, 0, 0, False)], sums=None)
    near, stack_other, sums, down = lax.optimization_barrier((near, stack_other, sums, down))
    near_other = sibling(near)
    sums = add([(stack_other, 0, 0, True), (near, 1, 0, False)], sums=sums)
    far, left, sums = lax.optimization_barrier((far, left, sums))
    far_other, left_other = sibling(far), sibling(left)
    sums = add([(near_other, 1, 0, True), (far, 2, 0, False), (left, 3, 0, False)], sums=sums)
    far_other, left_other, sums = lax.optimization_barrier((far_other, left_other, sums))
    hidden = add([(far_other, 2, 0, True), (left_other, 3, 0, True)], sums=sums, last=True)

    pieces = {}
    for outer in (1, 2, 3, 0):
        mine, others = down_pieces(place, hidden, down, outer, rows)
        if outer > 1:
            pieces[outer - 1], hidden = lax.optimization_barrier((pieces[outer - 1], hidden))
        pieces[outer] = mine + sibling(others).astype(F32)
    level = pieces[0]
    for d in range(1, SIDE):
        level = level + level_two(pieces[d].astype(BF16), d).astype(F32)
    total = level[0]
    for d in range(1, SIDE):
        total = total + level_one(level[d].astype(BF16), d).astype(F32)

    back = total[:, rows:].astype(BF16).T.reshape(experts, capacity, cols)
    returned = lax.all_to_all(back, "expert", 0, 0, tiled=True).reshape(experts * capacity, cols)
    moe_out = jnp.dot(combine.T, returned.astype(F32), precision=lax.Precision.HIGHEST)
    return (total[:, :rows].T + moe_out).astype(BF16)


def solution(mesh):
    in_specs = (
        P("expert", "tensor"),
        P(),
        P("expert", None),
        P("expert", None),
        P("tensor", None),
        P("tensor", None),
        P("tensor", None),
        P("expert", "tensor", None),
        P("expert", "tensor", None),
        P("expert", "tensor", None),
    )
    out_specs = P("expert", "tensor")
    return jax.shard_map(shards, mesh=mesh, in_specs=in_specs, out_specs=out_specs, check_vma=False)
```

```python
import functools

import jax
import jax.numpy as jnp
from jax import lax
from jax.experimental import pallas as pl
from jax.experimental.pallas import tpu as pltpu
from jax.sharding import PartitionSpec as P

SIDE = 4
PAIR = 2
CHIPS = SIDE * SIDE
GROUP = CHIPS * PAIR
F32 = jnp.float32
BF16 = jnp.bfloat16
MIB = 1024 * 1024
MOST = 56 * MIB
CHUNK = 896
SMALL = pl.CostEstimate(flops=MIB, bytes_accessed=MIB, transcendentals=0)


def device_of(x, y, core):
    return (x * SIDE + y) * PAIR + core


def hops(step, first):
    pairs = []
    for x in range(SIDE):
        for y in range(SIDE):
            for core in range(PAIR):
                along_x = (core == 0) == first
                to_x = (x + step) % SIDE if along_x else x
                to_y = y if along_x else (y + step) % SIDE
                pairs.append((device_of(x, y, core), device_of(to_x, to_y, core)))
    return pairs


def sibling(value):
    return lax.ppermute(value, "tensor", [(i, i ^ 1) for i in range(GROUP)])


def piece_index(place, other, sign, outer, inner):
    x, y, core = place[0], place[1], place[2]
    owner = 1 - core if other else core
    move_x = jnp.where(owner == 0, inner, outer)
    move_y = jnp.where(owner == 0, outer, inner)
    at_x = lax.rem(x + sign * move_x + SIDE, SIDE)
    at_y = lax.rem(y + sign * move_y + SIDE, SIDE)
    return device_of(at_x, at_y, owner)


def dispatch_kernel(experts, capacity, ids, probs, tokens, outgoing, combine):
    choose, rows = ids.shape
    slots = experts * capacity
    numbers = lax.broadcasted_iota(jnp.int32, (experts, rows), 0)
    before = lax.broadcasted_iota(jnp.int32, (rows, rows), 0)
    after = lax.broadcasted_iota(jnp.int32, (rows, rows), 1)
    earlier = (before < after).astype(F32).astype(BF16)
    slot_numbers = lax.broadcasted_iota(jnp.int32, (slots, rows), 0)
    taken = jnp.zeros((experts, 1), F32)
    weights = jnp.zeros((slots, rows), F32)
    chosen = jnp.zeros((slots, rows), F32)
    for k in range(choose):
        named = ids[k : k + 1, :]
        onehot = (numbers == named).astype(F32)
        ahead = jnp.dot(onehot.astype(BF16), earlier, preferred_element_type=F32) + taken
        position = jnp.sum(ahead * onehot, axis=0, keepdims=True).astype(jnp.int32)
        hits = slot_numbers == named * capacity + position
        weights = weights + jnp.where(hits, probs[k : k + 1, :], 0.0)
        chosen = chosen + hits.astype(F32)
        taken = taken + jnp.sum(onehot, axis=1, keepdims=True)
    combine[...] = weights
    outgoing[...] = lax.dot_general(
        chosen.astype(BF16), tokens[...], (((1,), (1,)), ((), ())), preferred_element_type=F32
    ).astype(BF16)


def dispatched(ids, probs, tokens, experts, capacity):
    cols, rows = tokens.shape
    return pl.pallas_call(
        functools.partial(dispatch_kernel, experts, capacity),
        out_shape=(
            jax.ShapeDtypeStruct((experts * capacity, cols), BF16),
            jax.ShapeDtypeStruct((experts * capacity, rows), F32),
        ),
        name="dispatch",
    )(ids, probs, tokens)


IN_HBM = pl.BlockSpec(memory_space=pl.ANY)
IN_VMEM = pl.BlockSpec(memory_space=pltpu.MemorySpace.VMEM)


def laid_out(form, cols, sources, out, held, pieces, arrived, gone):
    each = CHUNK // cols
    steps = pieces.shape[0] // each
    reads = [
        [
            pltpu.make_async_copy(
                source.at[:, step * CHUNK : (step + 1) * CHUNK],
                held.at[i, :, step * CHUNK : (step + 1) * CHUNK],
                arrived.at[i, step],
            )
            for i, source in enumerate(sources)
        ]
        for step in range(steps)
    ]
    writes = [
        pltpu.make_async_copy(
            pieces.at[step * each : (step + 1) * each],
            out.at[step * each : (step + 1) * each],
            gone.at[step],
        )
        for step in range(steps)
    ]
    for row in reads:
        for copy in row:
            copy.start()
    for step in range(steps):
        for copy in reads[step]:
            copy.wait()
        for i in range(step * each, (step + 1) * each):
            pieces[i] = form(held, slice(i * cols, (i + 1) * cols))
        writes[step].start()
    for copy in writes:
        copy.wait()


def up_weights_kernel(cols, gain, gate, up, out, held, pieces, arrived, gone):
    def form(held, at):
        both = jnp.concatenate([held[0, :, at].astype(F32), held[1, :, at].astype(F32)], axis=0)
        return (both * gain[:, at]).astype(BF16)

    laid_out(form, cols, [gate, up], out, held, pieces, arrived, gone)


def down_weights_kernel(cols, down, out, held, pieces, arrived, gone):
    def form(held, at):
        return held[0, :, at].astype(F32).T.astype(BF16)

    laid_out(form, cols, [down], out, held, pieces, arrived, gone)


def layout_call(kernel, name, cols, piece, sources, gain=()):
    units, width = sources[0].shape
    shape = (width // cols,) + piece
    return pl.pallas_call(
        functools.partial(kernel, cols),
        out_shape=jax.ShapeDtypeStruct(shape, BF16),
        in_specs=[IN_VMEM] * len(gain) + [IN_HBM] * len(sources),
        out_specs=IN_HBM,
        scratch_shapes=[
            pltpu.VMEM((len(sources), units, width), BF16),
            pltpu.VMEM(shape, BF16),
            pltpu.SemaphoreType.DMA((len(sources), width // CHUNK)),
            pltpu.SemaphoreType.DMA((width // CHUNK,)),
        ],
        compiler_params=pltpu.CompilerParams(vmem_limit_bytes=MOST),
        cost_estimate=SMALL,
        name=name,
    )(*gain, *sources)


def up_weights(gain, gate, up, cols):
    piece = (2 * gate.shape[0], cols)
    return layout_call(up_weights_kernel, "up_weights", cols, piece, [gate, up], [gain])


def down_weights(down, cols):
    return layout_call(down_weights_kernel, "down_weights", cols, (cols, down.shape[0]), [down])


def arrive_kernel(dense_rows, count, start, last, width, place, *refs):
    stacks, dense, routed = (refs[i * count : (i + 1) * count] for i in range(3))
    refs = refs[3 * count :]
    if not start:
        carried, refs = refs[:3], refs[3:]
    if last:
        hidden, refs = refs[0], refs[1:]
    dense_sum, routed_sum, squares = refs

    @pl.when(pl.program_id(0) == 0)
    def _():
        for i, ref in enumerate(refs):
            ref[...] = jnp.zeros_like(ref) if start else carried[i][...]

    for stack, dense_weight, routed_weight in zip(stacks, dense, routed):
        block = stack[0]
        dense_sum[...] += jnp.dot(
            dense_weight[0], block[:, :dense_rows], preferred_element_type=F32
        )
        routed_sum[...] += jnp.dot(
            routed_weight[0], block[:, dense_rows:], preferred_element_type=F32
        )
        values = block.astype(F32)
        values = values * values
        squares[...] += jnp.sum(values.reshape(values.shape[0] // 8, 8, values.shape[1]), axis=0)

    if last:

        @pl.when(pl.program_id(0) == pl.num_programs(0) - 1)
        def _():
            scale = lax.rsqrt(jnp.sum(squares[...], axis=0, keepdims=True) / width + 1e-05)
            units = dense_sum.shape[0] // 2
            for sums, span in (
                (dense_sum, slice(0, dense_rows)),
                (routed_sum, slice(dense_rows, scale.shape[1])),
            ):
                gates = sums[:units, :] * scale[:, span]
                ups = sums[units:, :] * scale[:, span]
                hidden[:, span] = (gates / (1.0 + jnp.exp(-gates)) * ups).astype(BF16)


def arrive(place, stage, weights, sums, dense_rows, last=False):
    count = len(stage)
    pieces, cols, rows = stage[0][0].shape
    height = weights[0].shape[1]
    start = sums is None

    def weight(outer, inner, other):
        def index(i, place):
            return piece_index(place, other, -1, outer, inner + i), 0, 0

        return pl.BlockSpec((1, height, cols), index)

    whole = lambda shape: pl.BlockSpec(shape, lambda i, place: (0, 0))
    shapes = [(height, dense_rows), (height, rows - dense_rows), (8, rows)]
    sum_specs = [whole(s) for s in shapes]
    if last:
        out_specs = whole((height // 2, rows))
        out_shape = jax.ShapeDtypeStruct((height // 2, rows), BF16)
        scratch = [pltpu.VMEM(s, F32) for s in shapes]
    else:
        out_specs, scratch = sum_specs, []
        out_shape = [jax.ShapeDtypeStruct(s, F32) for s in shapes]
    return pl.pallas_call(
        functools.partial(arrive_kernel, dense_rows, count, start, last, GROUP * cols),
        out_shape=out_shape,
        grid_spec=pltpu.PrefetchScalarGridSpec(
            num_scalar_prefetch=1,
            grid=(pieces,),
            in_specs=[pl.BlockSpec((1, cols, rows), lambda i, place: (i, 0, 0))] * count
            + [weight(*rest) for _, *rest in stage] * 2
            + ([] if start else sum_specs),
            out_specs=out_specs,
            scratch_shapes=scratch,
        ),
        compiler_params=pltpu.CompilerParams(vmem_limit_bytes=24 * MIB),
        cost_estimate=SMALL,
        name=f"arrive_{stage[-1][1]}_{count}",
    )(
        place,
        *[stack for stack, *_ in stage],
        *[weights[0]] * count,
        *[weights[1]] * count,
        *([] if start else sums),
    )


def down_kernel(dense_rows, place, hidden, dense, routed, out):
    for weight, span in (
        (dense, slice(0, dense_rows)),
        (routed, slice(dense_rows, hidden.shape[1])),
    ):
        out[0, :, span] = jnp.dot(
            weight[0], hidden[:, span], preferred_element_type=F32
        ).astype(out.dtype)


def down_pieces(place, hidden, weights, outer, other, dense_rows):
    units, rows = hidden.shape
    cols = weights[0].shape[1]
    weight = pl.BlockSpec(
        (1, cols, units), lambda i, place: (piece_index(place, other, 1, outer, i), 0, 0)
    )
    return pl.pallas_call(
        functools.partial(down_kernel, dense_rows),
        out_shape=jax.ShapeDtypeStruct((SIDE, cols, rows), BF16 if other else F32),
        grid_spec=pltpu.PrefetchScalarGridSpec(
            num_scalar_prefetch=1,
            grid=(SIDE,),
            in_specs=[pl.BlockSpec((units, rows), lambda i, place: (0, 0)), weight, weight],
            out_specs=pl.BlockSpec((1, cols, rows), lambda i, place: (i, 0, 0)),
        ),
        compiler_params=pltpu.CompilerParams(vmem_limit_bytes=16 * MIB),
        cost_estimate=SMALL,
        name=f"down_{'other' if other else 'mine'}_{outer}",
    )(place, hidden, weights[0], weights[1])


def shards(
    tokens,
    norm_gain,
    route_ids,
    route_probs,
    dense_gate,
    dense_up,
    dense_down,
    expert_gate,
    expert_up,
    expert_down,
):
    experts = lax.axis_size("expert")
    rows, choose = route_ids.shape
    cols = tokens.shape[1]
    capacity = 3 * rows * choose // (2 * experts)
    index = lax.axis_index("tensor")
    place = jnp.stack([index // (SIDE * PAIR), index // PAIR % SIDE, index % PAIR]).astype(jnp.int32)

    gain = norm_gain[None, :]

    outgoing, combine = dispatched(route_ids.T, route_probs.T, tokens.T, experts, capacity)
    received = lax.all_to_all(
        outgoing.reshape(experts, capacity, cols), "expert", 0, 0, tiled=True
    ).reshape(experts * capacity, cols)
    weights = [
        up_weights(gain, dense_gate, dense_up, cols),
        up_weights(gain, expert_gate[0], expert_up[0], cols),
    ]
    received, weights = lax.optimization_barrier((received, weights))
    own = jnp.concatenate([tokens.T, received.T], axis=1)

    def level_one(value, d):
        return lax.ppermute(value, "tensor", hops(d, True))

    def level_two(value, d):
        return lax.ppermute(value, "tensor", hops(d, False))

    arrived = [level_one(own, d) for d in range(1, SIDE)]
    routed_down = down_weights(expert_down[0], cols)
    arrived, routed_down = lax.optimization_barrier((arrived, routed_down))
    stack = jnp.stack([own] + arrived)
    near, far, left = [level_two(stack, d) for d in range(1, SIDE)]
    stack_other = sibling(stack)
    down = [down_weights(dense_down, cols), routed_down]
    add = functools.partial(arrive, place, weights=weights, dense_rows=rows)
    sums = add([(stack, 0, 0, False)], sums=None)
    near, stack_other, sums, down = lax.optimization_barrier((near, stack_other, sums, down))
    near_other = sibling(near)
    sums = add([(stack_other, 0, 0, True), (near, 1, 0, False)], sums=sums)
    far, left, sums = lax.optimization_barrier((far, left, sums))
    far_other, left_other = sibling(far), sibling(left)
    sums = add([(near_other, 1, 0, True), (far, 2, 0, False), (left, 3, 0, False)], sums=sums)
    far_other, left_other, sums = lax.optimization_barrier((far_other, left_other, sums))
    hidden = add([(far_other, 2, 0, True), (left_other, 3, 0, True)], sums=sums, last=True)

    def shares(outer, other, hidden):
        out = down_pieces(place, hidden, down, outer, other, rows)
        return lax.optimization_barrier((out, hidden))

    pieces, order = {}, (2, 1, 3)
    for d in order:
        pieces[d], hidden = shares(d, True, hidden)
    pieces = {d: sibling(pieces[d]) for d in order}
    for d in order:
        mine, hidden = shares(d, False, hidden)
        pieces[d] = (mine + pieces[d].astype(F32)).astype(BF16)
    pieces, hidden = lax.optimization_barrier((pieces, hidden))
    others, hidden = shares(0, True, hidden)
    mine, hidden = shares(0, False, hidden)
    level = mine + sibling(others).astype(F32)
    for d in order:
        level = level + level_two(pieces[d], d).astype(F32)
    total = level[0]
    for d in order:
        total = total + level_one(level[d].astype(BF16), d).astype(F32)

    back = total[:, rows:].astype(BF16).T.reshape(experts, capacity, cols)
    returned = lax.all_to_all(back, "expert", 0, 0, tiled=True).reshape(experts * capacity, cols)
    moe_out = jnp.dot(combine.T, returned.astype(F32), precision=lax.Precision.HIGHEST)
    return (total[:, :rows].T + moe_out).astype(BF16)


def solution(mesh):
    in_specs = (
        P("expert", "tensor"),
        P(),
        P("expert", None),
        P("expert", None),
        P("tensor", None),
        P("tensor", None),
        P("tensor", None),
        P("expert", "tensor", None),
        P("expert", "tensor", None),
        P("expert", "tensor", None),
    )
    out_specs = P("expert", "tensor")
    return jax.shard_map(shards, mesh=mesh, in_specs=in_specs, out_specs=out_specs, check_vma=False)
```

```python
import functools

import jax
import jax.numpy as jnp
from jax import lax
from jax.experimental import pallas as pl
from jax.experimental.pallas import tpu as pltpu
from jax.sharding import PartitionSpec as P

SIDE = 4
PAIR = 2
CHIPS = SIDE * SIDE
GROUP = CHIPS * PAIR
F32 = jnp.float32
BF16 = jnp.bfloat16
MIB = 1024 * 1024
MOST = 56 * MIB
CHUNK = 896
SMALL = pl.CostEstimate(flops=MIB, bytes_accessed=MIB, transcendentals=0)


def device_of(x, y, core):
    return (x * SIDE + y) * PAIR + core


def hops(step, first):
    pairs = []
    for x in range(SIDE):
        for y in range(SIDE):
            for core in range(PAIR):
                along_x = (core == 0) == first
                to_x = (x + step) % SIDE if along_x else x
                to_y = y if along_x else (y + step) % SIDE
                pairs.append((device_of(x, y, core), device_of(to_x, to_y, core)))
    return pairs


def sibling(value):
    return lax.ppermute(value, "tensor", [(i, i ^ 1) for i in range(GROUP)])


def piece_index(place, other, sign, outer, inner):
    x, y, core = place[0], place[1], place[2]
    owner = 1 - core if other else core
    move_x = jnp.where(owner == 0, inner, outer)
    move_y = jnp.where(owner == 0, outer, inner)
    at_x = lax.rem(x + sign * move_x + SIDE, SIDE)
    at_y = lax.rem(y + sign * move_y + SIDE, SIDE)
    return device_of(at_x, at_y, owner)


def dispatch_kernel(experts, capacity, ids, probs, tokens, outgoing, combine):
    choose, rows = ids.shape
    slots = experts * capacity
    numbers = lax.broadcasted_iota(jnp.int32, (experts, rows), 0)
    before = lax.broadcasted_iota(jnp.int32, (rows, rows), 0)
    after = lax.broadcasted_iota(jnp.int32, (rows, rows), 1)
    earlier = (before < after).astype(F32).astype(BF16)
    slot_numbers = lax.broadcasted_iota(jnp.int32, (slots, rows), 0)
    taken = jnp.zeros((experts, 1), F32)
    weights = jnp.zeros((slots, rows), F32)
    chosen = jnp.zeros((slots, rows), F32)
    for k in range(choose):
        named = ids[k : k + 1, :]
        onehot = (numbers == named).astype(F32)
        ahead = jnp.dot(onehot.astype(BF16), earlier, preferred_element_type=F32) + taken
        position = jnp.sum(ahead * onehot, axis=0, keepdims=True).astype(jnp.int32)
        hits = slot_numbers == named * capacity + position
        weights = weights + jnp.where(hits, probs[k : k + 1, :], 0.0)
        chosen = chosen + hits.astype(F32)
        taken = taken + jnp.sum(onehot, axis=1, keepdims=True)
    combine[...] = weights
    outgoing[...] = lax.dot_general(
        chosen.astype(BF16), tokens[...], (((1,), (1,)), ((), ())), preferred_element_type=F32
    ).astype(BF16)


def dispatched(ids, probs, tokens, experts, capacity):
    cols, rows = tokens.shape
    return pl.pallas_call(
        functools.partial(dispatch_kernel, experts, capacity),
        out_shape=(
            jax.ShapeDtypeStruct((experts * capacity, cols), BF16),
            jax.ShapeDtypeStruct((experts * capacity, rows), F32),
        ),
        name="dispatch",
    )(ids, probs, tokens)


IN_HBM = pl.BlockSpec(memory_space=pl.ANY)
IN_VMEM = pl.BlockSpec(memory_space=pltpu.MemorySpace.VMEM)


def laid_out(form, cols, sources, out, held, pieces, arrived, gone):
    each = CHUNK // cols
    steps = pieces.shape[0] // each
    reads = [
        [
            pltpu.make_async_copy(
                source.at[:, step * CHUNK : (step + 1) * CHUNK],
                held.at[i, :, step * CHUNK : (step + 1) * CHUNK],
                arrived.at[i, step],
            )
            for i, source in enumerate(sources)
        ]
        for step in range(steps)
    ]
    writes = [
        pltpu.make_async_copy(
            pieces.at[step * each : (step + 1) * each],
            out.at[step * each : (step + 1) * each],
            gone.at[step],
        )
        for step in range(steps)
    ]
    for row in reads:
        for copy in row:
            copy.start()
    for step in range(steps):
        for copy in reads[step]:
            copy.wait()
        for i in range(step * each, (step + 1) * each):
            pieces[i] = form(held, slice(i * cols, (i + 1) * cols))
        writes[step].start()
    for copy in writes:
        copy.wait()


def up_weights_kernel(cols, gain, gate, up, out, held, pieces, arrived, gone):
    def form(held, at):
        both = jnp.concatenate([held[0, :, at].astype(F32), held[1, :, at].astype(F32)], axis=0)
        return (both * gain[:, at]).astype(BF16)

    laid_out(form, cols, [gate, up], out, held, pieces, arrived, gone)


def down_weights_kernel(cols, down, out, held, pieces, arrived, gone):
    def form(held, at):
        return held[0, :, at].astype(F32).T.astype(BF16)

    laid_out(form, cols, [down], out, held, pieces, arrived, gone)


def layout_call(kernel, name, cols, piece, sources, gain=()):
    units, width = sources[0].shape
    shape = (width // cols,) + piece
    return pl.pallas_call(
        functools.partial(kernel, cols),
        out_shape=jax.ShapeDtypeStruct(shape, BF16),
        in_specs=[IN_VMEM] * len(gain) + [IN_HBM] * len(sources),
        out_specs=IN_HBM,
        scratch_shapes=[
            pltpu.VMEM((len(sources), units, width), BF16),
            pltpu.VMEM(shape, BF16),
            pltpu.SemaphoreType.DMA((len(sources), width // CHUNK)),
            pltpu.SemaphoreType.DMA((width // CHUNK,)),
        ],
        compiler_params=pltpu.CompilerParams(vmem_limit_bytes=MOST),
        cost_estimate=SMALL,
        name=name,
    )(*gain, *sources)


def up_weights(gain, gate, up, cols):
    piece = (2 * gate.shape[0], cols)
    return layout_call(up_weights_kernel, "up_weights", cols, piece, [gate, up], [gain])


def down_weights(down, cols):
    return layout_call(down_weights_kernel, "down_weights", cols, (cols, down.shape[0]), [down])


def arrive_kernel(dense_rows, count, start, last, width, place, *refs):
    stacks, dense, routed = (refs[i * count : (i + 1) * count] for i in range(3))
    refs = refs[3 * count :]
    if not start:
        carried, refs = refs[:3], refs[3:]
    if last:
        hidden, refs = refs[0], refs[1:]
    dense_sum, routed_sum, squares = refs

    @pl.when(pl.program_id(0) == 0)
    def _():
        for i, ref in enumerate(refs):
            ref[...] = jnp.zeros_like(ref) if start else carried[i][...]

    for stack, dense_weight, routed_weight in zip(stacks, dense, routed):
        block = stack[0]
        dense_sum[...] += jnp.dot(
            dense_weight[0], block[:, :dense_rows], preferred_element_type=F32
        )
        routed_sum[...] += jnp.dot(
            routed_weight[0], block[:, dense_rows:], preferred_element_type=F32
        )
        values = block.astype(F32)
        values = values * values
        squares[...] += jnp.sum(values.reshape(values.shape[0] // 8, 8, values.shape[1]), axis=0)

    if last:

        @pl.when(pl.program_id(0) == pl.num_programs(0) - 1)
        def _():
            scale = lax.rsqrt(jnp.sum(squares[...], axis=0, keepdims=True) / width + 1e-05)
            units = dense_sum.shape[0] // 2
            for sums, span in (
                (dense_sum, slice(0, dense_rows)),
                (routed_sum, slice(dense_rows, scale.shape[1])),
            ):
                gates = sums[:units, :] * scale[:, span]
                ups = sums[units:, :] * scale[:, span]
                hidden[:, span] = (gates / (1.0 + jnp.exp(-gates)) * ups).astype(BF16)


def arrive(place, stage, weights, sums, dense_rows, last=False):
    count = len(stage)
    pieces, cols, rows = stage[0][0].shape
    height = weights[0].shape[1]
    start = sums is None

    def weight(outer, inner, other):
        def index(i, place):
            return piece_index(place, other, -1, outer, inner + i), 0, 0

        return pl.BlockSpec((1, height, cols), index)

    whole = lambda shape: pl.BlockSpec(shape, lambda i, place: (0, 0))
    shapes = [(height, dense_rows), (height, rows - dense_rows), (8, rows)]
    sum_specs = [whole(s) for s in shapes]
    if last:
        out_specs = whole((height // 2, rows))
        out_shape = jax.ShapeDtypeStruct((height // 2, rows), BF16)
        scratch = [pltpu.VMEM(s, F32) for s in shapes]
    else:
        out_specs, scratch = sum_specs, []
        out_shape = [jax.ShapeDtypeStruct(s, F32) for s in shapes]
    return pl.pallas_call(
        functools.partial(arrive_kernel, dense_rows, count, start, last, GROUP * cols),
        out_shape=out_shape,
        grid_spec=pltpu.PrefetchScalarGridSpec(
            num_scalar_prefetch=1,
            grid=(pieces,),
            in_specs=[pl.BlockSpec((1, cols, rows), lambda i, place: (i, 0, 0))] * count
            + [weight(*rest) for _, *rest in stage] * 2
            + ([] if start else sum_specs),
            out_specs=out_specs,
            scratch_shapes=scratch,
        ),
        compiler_params=pltpu.CompilerParams(vmem_limit_bytes=24 * MIB),
        cost_estimate=SMALL,
        name=f"arrive_{stage[-1][1]}_{count}",
    )(
        place,
        *[stack for stack, *_ in stage],
        *[weights[0]] * count,
        *[weights[1]] * count,
        *([] if start else sums),
    )


def down_kernel(dense_rows, place, hidden, *refs):
    mine, others = refs[4:]
    for out, dense, routed in ((mine, refs[0], refs[1]), (others, refs[2], refs[3])):
        for weight, span in (
            (dense, slice(0, dense_rows)),
            (routed, slice(dense_rows, hidden.shape[1])),
        ):
            out[0, :, span] = jnp.dot(
                weight[0], hidden[:, span], preferred_element_type=F32
            ).astype(out.dtype)


def down_pieces(place, hidden, weights, outer, dense_rows):
    units, rows = hidden.shape
    cols = weights[0].shape[1]

    def weight(other):
        def index(i, place):
            return piece_index(place, other, 1, outer, i), 0, 0

        return pl.BlockSpec((1, cols, units), index)

    out = pl.BlockSpec((1, cols, rows), lambda i, place: (i, 0, 0))
    shape = (SIDE, cols, rows)
    return pl.pallas_call(
        functools.partial(down_kernel, dense_rows),
        out_shape=(jax.ShapeDtypeStruct(shape, F32), jax.ShapeDtypeStruct(shape, BF16)),
        grid_spec=pltpu.PrefetchScalarGridSpec(
            num_scalar_prefetch=1,
            grid=(SIDE,),
            in_specs=[pl.BlockSpec((units, rows), lambda i, place: (0, 0))]
            + [weight(False)] * 2
            + [weight(True)] * 2,
            out_specs=(out, out),
        ),
        compiler_params=pltpu.CompilerParams(vmem_limit_bytes=16 * MIB),
        cost_estimate=SMALL,
        name=f"down_pieces_{outer}",
    )(place, hidden, weights[0], weights[1], weights[0], weights[1])


def shards(
    tokens,
    norm_gain,
    route_ids,
    route_probs,
    dense_gate,
    dense_up,
    dense_down,
    expert_gate,
    expert_up,
    expert_down,
):
    experts = lax.axis_size("expert")
    rows, choose = route_ids.shape
    cols = tokens.shape[1]
    capacity = 3 * rows * choose // (2 * experts)
    index = lax.axis_index("tensor")
    place = jnp.stack([index // (SIDE * PAIR), index // PAIR % SIDE, index % PAIR]).astype(jnp.int32)

    gain = norm_gain[None, :]

    outgoing, combine = dispatched(route_ids.T, route_probs.T, tokens.T, experts, capacity)
    received = lax.all_to_all(
        outgoing.reshape(experts, capacity, cols), "expert", 0, 0, tiled=True
    ).reshape(experts * capacity, cols)
    weights = [
        up_weights(gain, dense_gate, dense_up, cols),
        up_weights(gain, expert_gate[0], expert_up[0], cols),
    ]
    received, weights = lax.optimization_barrier((received, weights))
    own = jnp.concatenate([tokens.T, received.T], axis=1)

    def level_one(value, d):
        return lax.ppermute(value, "tensor", hops(d, True))

    def level_two(value, d):
        return lax.ppermute(value, "tensor", hops(d, False))

    arrived = [level_one(own, d) for d in range(1, SIDE)]
    routed_down = down_weights(expert_down[0], cols)
    arrived, routed_down = lax.optimization_barrier((arrived, routed_down))
    stack = jnp.stack([own] + arrived)
    near, far, left = [level_two(stack, d) for d in range(1, SIDE)]
    stack_other = sibling(stack)
    down = [down_weights(dense_down, cols), routed_down]
    add = functools.partial(arrive, place, weights=weights, dense_rows=rows)
    sums = add([(stack, 0, 0, False)], sums=None)
    near, stack_other, sums, down = lax.optimization_barrier((near, stack_other, sums, down))
    near_other = sibling(near)
    sums = add([(stack_other, 0, 0, True), (near, 1, 0, False)], sums=sums)
    far, left, sums = lax.optimization_barrier((far, left, sums))
    far_other, left_other = sibling(far), sibling(left)
    sums = add([(near_other, 1, 0, True), (far, 2, 0, False), (left, 3, 0, False)], sums=sums)
    far_other, left_other, sums = lax.optimization_barrier((far_other, left_other, sums))
    hidden = add([(far_other, 2, 0, True), (left_other, 3, 0, True)], sums=sums, last=True)

    pieces, order = {}, (2, 1, 3, 0)
    for i, outer in enumerate(order):
        mine, others = down_pieces(place, hidden, down, outer, rows)
        if i > 0:
            before = order[i - 1]
            pieces[before], hidden = lax.optimization_barrier((pieces[before], hidden))
        pieces[outer] = mine + sibling(others).astype(F32)
    level = pieces[0]
    for d in order[:-1]:
        level = level + level_two(pieces[d].astype(BF16), d).astype(F32)
    total = level[0]
    for d in order[:-1]:
        total = total + level_one(level[d].astype(BF16), d).astype(F32)

    back = total[:, rows:].astype(BF16).T.reshape(experts, capacity, cols)
    returned = lax.all_to_all(back, "expert", 0, 0, tiled=True).reshape(experts * capacity, cols)
    moe_out = jnp.dot(combine.T, returned.astype(F32), precision=lax.Precision.HIGHEST)
    return (total[:, :rows].T + moe_out).astype(BF16)


def solution(mesh):
    in_specs = (
        P("expert", "tensor"),
        P(),
        P("expert", None),
        P("expert", None),
        P("tensor", None),
        P("tensor", None),
        P("tensor", None),
        P("expert", "tensor", None),
        P("expert", "tensor", None),
        P("expert", "tensor", None),
    )
    out_specs = P("expert", "tensor")
    return jax.shard_map(shards, mesh=mesh, in_specs=in_specs, out_specs=out_specs, check_vma=False)
```

```python
import functools

import jax
import jax.numpy as jnp
from jax import lax
from jax.experimental import pallas as pl
from jax.experimental.pallas import tpu as pltpu
from jax.sharding import PartitionSpec as P

SIDE = 4
PAIR = 2
CHIPS = SIDE * SIDE
GROUP = CHIPS * PAIR
F32 = jnp.float32
BF16 = jnp.bfloat16
MIB = 1024 * 1024
MOST = 56 * MIB
CHUNK = 896
SMALL = pl.CostEstimate(flops=MIB, bytes_accessed=MIB, transcendentals=0)


def device_of(x, y, core):
    return (x * SIDE + y) * PAIR + core


def hops(step, first):
    pairs = []
    for x in range(SIDE):
        for y in range(SIDE):
            for core in range(PAIR):
                along_x = (core == 0) == first
                to_x = (x + step) % SIDE if along_x else x
                to_y = y if along_x else (y + step) % SIDE
                pairs.append((device_of(x, y, core), device_of(to_x, to_y, core)))
    return pairs


def sibling(value):
    return lax.ppermute(value, "tensor", [(i, i ^ 1) for i in range(GROUP)])


def piece_index(place, other, sign, outer, inner):
    x, y, core = place[0], place[1], place[2]
    owner = 1 - core if other else core
    move_x = jnp.where(owner == 0, inner, outer)
    move_y = jnp.where(owner == 0, outer, inner)
    at_x = lax.rem(x + sign * move_x + SIDE, SIDE)
    at_y = lax.rem(y + sign * move_y + SIDE, SIDE)
    return device_of(at_x, at_y, owner)


def dispatch_kernel(experts, capacity, ids, probs, tokens, outgoing, combine):
    choose, rows = ids.shape
    slots = experts * capacity
    numbers = lax.broadcasted_iota(jnp.int32, (experts, rows), 0)
    before = lax.broadcasted_iota(jnp.int32, (rows, rows), 0)
    after = lax.broadcasted_iota(jnp.int32, (rows, rows), 1)
    earlier = (before < after).astype(F32).astype(BF16)
    slot_numbers = lax.broadcasted_iota(jnp.int32, (slots, rows), 0)
    taken = jnp.zeros((experts, 1), F32)
    weights = jnp.zeros((slots, rows), F32)
    chosen = jnp.zeros((slots, rows), F32)
    for k in range(choose):
        named = ids[k : k + 1, :]
        onehot = (numbers == named).astype(F32)
        ahead = jnp.dot(onehot.astype(BF16), earlier, preferred_element_type=F32) + taken
        position = jnp.sum(ahead * onehot, axis=0, keepdims=True).astype(jnp.int32)
        hits = slot_numbers == named * capacity + position
        weights = weights + jnp.where(hits, probs[k : k + 1, :], 0.0)
        chosen = chosen + hits.astype(F32)
        taken = taken + jnp.sum(onehot, axis=1, keepdims=True)
    combine[...] = weights
    outgoing[...] = lax.dot_general(
        chosen.astype(BF16), tokens[...], (((1,), (1,)), ((), ())), preferred_element_type=F32
    ).astype(BF16)


def dispatched(ids, probs, tokens, experts, capacity):
    cols, rows = tokens.shape
    return pl.pallas_call(
        functools.partial(dispatch_kernel, experts, capacity),
        out_shape=(
            jax.ShapeDtypeStruct((experts * capacity, cols), BF16),
            jax.ShapeDtypeStruct((experts * capacity, rows), F32),
        ),
        name="dispatch",
    )(ids, probs, tokens)


IN_HBM = pl.BlockSpec(memory_space=pl.ANY)
IN_VMEM = pl.BlockSpec(memory_space=pltpu.MemorySpace.VMEM)


def laid_out(form, cols, sources, out, held, pieces, arrived, gone):
    each = CHUNK // cols
    steps = pieces.shape[0] // each
    reads = [
        [
            pltpu.make_async_copy(
                source.at[:, step * CHUNK : (step + 1) * CHUNK],
                held.at[i, :, step * CHUNK : (step + 1) * CHUNK],
                arrived.at[i, step],
            )
            for i, source in enumerate(sources)
        ]
        for step in range(steps)
    ]
    writes = [
        pltpu.make_async_copy(
            pieces.at[step * each : (step + 1) * each],
            out.at[step * each : (step + 1) * each],
            gone.at[step],
        )
        for step in range(steps)
    ]
    for row in reads:
        for copy in row:
            copy.start()
    for step in range(steps):
        for copy in reads[step]:
            copy.wait()
        for i in range(step * each, (step + 1) * each):
            pieces[i] = form(held, slice(i * cols, (i + 1) * cols))
        writes[step].start()
    for copy in writes:
        copy.wait()


def up_weights_kernel(cols, gain, gate, up, out, held, pieces, arrived, gone):
    def form(held, at):
        both = jnp.concatenate([held[0, :, at].astype(F32), held[1, :, at].astype(F32)], axis=0)
        return (both * gain[:, at]).astype(BF16)

    laid_out(form, cols, [gate, up], out, held, pieces, arrived, gone)


def down_weights_kernel(cols, down, out, held, pieces, arrived, gone):
    def form(held, at):
        return held[0, :, at].astype(F32).T.astype(BF16)

    laid_out(form, cols, [down], out, held, pieces, arrived, gone)


def layout_call(kernel, name, cols, piece, sources, gain=()):
    units, width = sources[0].shape
    shape = (width // cols,) + piece
    return pl.pallas_call(
        functools.partial(kernel, cols),
        out_shape=jax.ShapeDtypeStruct(shape, BF16),
        in_specs=[IN_VMEM] * len(gain) + [IN_HBM] * len(sources),
        out_specs=IN_HBM,
        scratch_shapes=[
            pltpu.VMEM((len(sources), units, width), BF16),
            pltpu.VMEM(shape, BF16),
            pltpu.SemaphoreType.DMA((len(sources), width // CHUNK)),
            pltpu.SemaphoreType.DMA((width // CHUNK,)),
        ],
        compiler_params=pltpu.CompilerParams(vmem_limit_bytes=MOST),
        cost_estimate=SMALL,
        name=name,
    )(*gain, *sources)


def up_weights(gain, gate, up, cols):
    piece = (2 * gate.shape[0], cols)
    return layout_call(up_weights_kernel, "up_weights", cols, piece, [gate, up], [gain])


def down_weights(down, cols):
    return layout_call(down_weights_kernel, "down_weights", cols, (cols, down.shape[0]), [down])


def arrive_kernel(dense_rows, count, start, last, width, place, *refs):
    stacks, dense, routed = (refs[i * count : (i + 1) * count] for i in range(3))
    refs = refs[3 * count :]
    if not start:
        carried, refs = refs[:3], refs[3:]
    if last:
        hidden, refs = refs[0], refs[1:]
    dense_sum, routed_sum, squares = refs

    @pl.when(pl.program_id(0) == 0)
    def _():
        for i, ref in enumerate(refs):
            ref[...] = jnp.zeros_like(ref) if start else carried[i][...]

    for stack, dense_weight, routed_weight in zip(stacks, dense, routed):
        block = stack[0]
        dense_sum[...] += jnp.dot(
            dense_weight[0], block[:, :dense_rows], preferred_element_type=F32
        )
        routed_sum[...] += jnp.dot(
            routed_weight[0], block[:, dense_rows:], preferred_element_type=F32
        )
        values = block.astype(F32)
        values = values * values
        squares[...] += jnp.sum(values.reshape(values.shape[0] // 8, 8, values.shape[1]), axis=0)

    if last:

        @pl.when(pl.program_id(0) == pl.num_programs(0) - 1)
        def _():
            scale = lax.rsqrt(jnp.sum(squares[...], axis=0, keepdims=True) / width + 1e-05)
            units = dense_sum.shape[0] // 2
            for sums, span in (
                (dense_sum, slice(0, dense_rows)),
                (routed_sum, slice(dense_rows, scale.shape[1])),
            ):
                gates = sums[:units, :] * scale[:, span]
                ups = sums[units:, :] * scale[:, span]
                hidden[:, span] = (gates / (1.0 + jnp.exp(-gates)) * ups).astype(BF16)


def arrive(place, stage, weights, sums, dense_rows, last=False):
    count = len(stage)
    pieces, cols, rows = stage[0][0].shape
    height = weights[0].shape[1]
    start = sums is None

    def weight(outer, inner, other):
        def index(i, place):
            return piece_index(place, other, -1, outer, inner + i), 0, 0

        return pl.BlockSpec((1, height, cols), index)

    whole = lambda shape: pl.BlockSpec(shape, lambda i, place: (0, 0))
    shapes = [(height, dense_rows), (height, rows - dense_rows), (8, rows)]
    sum_specs = [whole(s) for s in shapes]
    if last:
        out_specs = whole((height // 2, rows))
        out_shape = jax.ShapeDtypeStruct((height // 2, rows), BF16)
        scratch = [pltpu.VMEM(s, F32) for s in shapes]
    else:
        out_specs, scratch = sum_specs, []
        out_shape = [jax.ShapeDtypeStruct(s, F32) for s in shapes]
    return pl.pallas_call(
        functools.partial(arrive_kernel, dense_rows, count, start, last, GROUP * cols),
        out_shape=out_shape,
        grid_spec=pltpu.PrefetchScalarGridSpec(
            num_scalar_prefetch=1,
            grid=(pieces,),
            in_specs=[pl.BlockSpec((1, cols, rows), lambda i, place: (i, 0, 0))] * count
            + [weight(*rest) for _, *rest in stage] * 2
            + ([] if start else sum_specs),
            out_specs=out_specs,
            scratch_shapes=scratch,
        ),
        compiler_params=pltpu.CompilerParams(vmem_limit_bytes=24 * MIB),
        cost_estimate=SMALL,
        name=f"arrive_{stage[-1][1]}_{count}",
    )(
        place,
        *[stack for stack, *_ in stage],
        *[weights[0]] * count,
        *[weights[1]] * count,
        *([] if start else sums),
    )


def down_kernel(dense_rows, place, hidden, *refs):
    mine, others = refs[4:]
    for out, dense, routed in ((mine, refs[0], refs[1]), (others, refs[2], refs[3])):
        for weight, span in (
            (dense, slice(0, dense_rows)),
            (routed, slice(dense_rows, hidden.shape[1])),
        ):
            out[0, :, span] = jnp.dot(
                weight[0], hidden[:, span], preferred_element_type=F32
            ).astype(out.dtype)


def down_pieces(place, hidden, weights, outer, dense_rows):
    units, rows = hidden.shape
    cols = weights[0].shape[1]

    def weight(other):
        def index(i, place):
            return piece_index(place, other, 1, outer, i), 0, 0

        return pl.BlockSpec((1, cols, units), index)

    out = pl.BlockSpec((1, cols, rows), lambda i, place: (i, 0, 0))
    shape = (SIDE, cols, rows)
    return pl.pallas_call(
        functools.partial(down_kernel, dense_rows),
        out_shape=(jax.ShapeDtypeStruct(shape, F32), jax.ShapeDtypeStruct(shape, BF16)),
        grid_spec=pltpu.PrefetchScalarGridSpec(
            num_scalar_prefetch=1,
            grid=(SIDE,),
            in_specs=[pl.BlockSpec((units, rows), lambda i, place: (0, 0))]
            + [weight(False)] * 2
            + [weight(True)] * 2,
            out_specs=(out, out),
        ),
        compiler_params=pltpu.CompilerParams(vmem_limit_bytes=16 * MIB),
        cost_estimate=SMALL,
        name=f"down_pieces_{outer}",
    )(place, hidden, weights[0], weights[1], weights[0], weights[1])


def shards(
    tokens,
    norm_gain,
    route_ids,
    route_probs,
    dense_gate,
    dense_up,
    dense_down,
    expert_gate,
    expert_up,
    expert_down,
):
    experts = lax.axis_size("expert")
    rows, choose = route_ids.shape
    cols = tokens.shape[1]
    capacity = 3 * rows * choose // (2 * experts)
    index = lax.axis_index("tensor")
    place = jnp.stack([index // (SIDE * PAIR), index // PAIR % SIDE, index % PAIR]).astype(jnp.int32)

    gain = norm_gain[None, :]

    outgoing, combine = dispatched(route_ids.T, route_probs.T, tokens.T, experts, capacity)
    received = lax.all_to_all(
        outgoing.reshape(experts, capacity, cols), "expert", 0, 0, tiled=True
    ).reshape(experts * capacity, cols)
    weights = [
        up_weights(gain, dense_gate, dense_up, cols),
        up_weights(gain, expert_gate[0], expert_up[0], cols),
    ]
    received, weights = lax.optimization_barrier((received, weights))
    own = jnp.concatenate([tokens.T, received.T], axis=1)

    def level_one(value, d):
        return lax.ppermute(value, "tensor", hops(d, True))

    def level_two(value, d):
        return lax.ppermute(value, "tensor", hops(d, False))

    arrived = [level_one(own, d) for d in range(1, SIDE)]
    routed_down = down_weights(expert_down[0], cols)
    arrived, routed_down = lax.optimization_barrier((arrived, routed_down))
    stack = jnp.stack([own] + arrived)
    near, far, left = [level_two(stack, d) for d in range(1, SIDE)]
    stack_other = sibling(stack)
    down = [down_weights(dense_down, cols), routed_down]
    add = functools.partial(arrive, place, weights=weights, dense_rows=rows)
    sums = add([(stack, 0, 0, False)], sums=None)
    near, stack_other, sums, down = lax.optimization_barrier((near, stack_other, sums, down))
    near_other = sibling(near)
    sums = add([(stack_other, 0, 0, True), (near, 1, 0, False)], sums=sums)
    far, left, sums = lax.optimization_barrier((far, left, sums))
    far_other, left_other = sibling(far), sibling(left)
    sums = add([(near_other, 1, 0, True), (far, 2, 0, False), (left, 3, 0, False)], sums=sums)
    far_other, left_other, sums = lax.optimization_barrier((far_other, left_other, sums))
    hidden = add([(far_other, 2, 0, True), (left_other, 3, 0, True)], sums=sums, last=True)

    pieces, order = {}, (2, 1, 3, 0)
    for i, outer in enumerate(order):
        mine, others = down_pieces(place, hidden, down, outer, rows)
        if i > 0:
            before = order[i - 1]
            pieces[before], hidden = lax.optimization_barrier((pieces[before], hidden))
        pieces[outer] = mine + sibling(others).astype(F32)
    def second(parts):
        level = parts[0]
        for d in order[:-1]:
            level = level + level_two(parts[d].astype(BF16), d).astype(F32)
        return level

    def first(level):
        return [level_one(level[d].astype(BF16), d) for d in order[:-1]]

    level = second({d: part[:, :, rows:] for d, part in pieces.items()})
    dense_parts = {d: part[:, :, :rows] for d, part in pieces.items()}
    level, dense_parts = lax.optimization_barrier((level, dense_parts))
    arrived = first(level)
    dense_level = second(dense_parts)
    total = level[0]
    for part in arrived:
        total = total + part.astype(F32)
    back = total.astype(BF16).T.reshape(experts, capacity, cols)
    returned = lax.all_to_all(back, "expert", 0, 0, tiled=True).reshape(experts * capacity, cols)
    dense_total = dense_level[0]
    for part in first(dense_level):
        dense_total = dense_total + part.astype(F32)

    moe_out = jnp.dot(combine.T, returned.astype(F32), precision=lax.Precision.HIGHEST)
    return (dense_total.T + moe_out).astype(BF16)


def solution(mesh):
    in_specs = (
        P("expert", "tensor"),
        P(),
        P("expert", None),
        P("expert", None),
        P("tensor", None),
        P("tensor", None),
        P("tensor", None),
        P("expert", "tensor", None),
        P("expert", "tensor", None),
        P("expert", "tensor", None),
    )
    out_specs = P("expert", "tensor")
    return jax.shard_map(shards, mesh=mesh, in_specs=in_specs, out_specs=out_specs, check_vma=False)
```

```python
import functools

import jax
import jax.numpy as jnp
from jax import lax
from jax.experimental import pallas as pl
from jax.experimental.pallas import tpu as pltpu
from jax.sharding import PartitionSpec as P

SIDE = 4
PAIR = 2
CHIPS = SIDE * SIDE
GROUP = CHIPS * PAIR
F32 = jnp.float32
BF16 = jnp.bfloat16
MIB = 1024 * 1024
MOST = 56 * MIB
CHUNK = 896
SMALL = pl.CostEstimate(flops=MIB, bytes_accessed=MIB, transcendentals=0)


def device_of(x, y, core):
    return (x * SIDE + y) * PAIR + core


def hops(step, first):
    pairs = []
    for x in range(SIDE):
        for y in range(SIDE):
            for core in range(PAIR):
                along_x = (core == 0) == first
                to_x = (x + step) % SIDE if along_x else x
                to_y = y if along_x else (y + step) % SIDE
                pairs.append((device_of(x, y, core), device_of(to_x, to_y, core)))
    return pairs


def sibling(value):
    return lax.ppermute(value, "tensor", [(i, i ^ 1) for i in range(GROUP)])


def piece_index(place, other, sign, outer, inner):
    x, y, core = place[0], place[1], place[2]
    owner = 1 - core if other else core
    move_x = jnp.where(owner == 0, inner, outer)
    move_y = jnp.where(owner == 0, outer, inner)
    at_x = lax.rem(x + sign * move_x + SIDE, SIDE)
    at_y = lax.rem(y + sign * move_y + SIDE, SIDE)
    return device_of(at_x, at_y, owner)


def dispatch_kernel(experts, capacity, ids, probs, tokens, outgoing, combine):
    choose, rows = ids.shape
    slots = experts * capacity
    numbers = lax.broadcasted_iota(jnp.int32, (experts, rows), 0)
    before = lax.broadcasted_iota(jnp.int32, (rows, rows), 0)
    after = lax.broadcasted_iota(jnp.int32, (rows, rows), 1)
    earlier = (before < after).astype(F32).astype(BF16)
    slot_numbers = lax.broadcasted_iota(jnp.int32, (slots, rows), 0)
    taken = jnp.zeros((experts, 1), F32)
    weights = jnp.zeros((slots, rows), F32)
    chosen = jnp.zeros((slots, rows), F32)
    for k in range(choose):
        named = ids[k : k + 1, :]
        onehot = (numbers == named).astype(F32)
        ahead = jnp.dot(onehot.astype(BF16), earlier, preferred_element_type=F32) + taken
        position = jnp.sum(ahead * onehot, axis=0, keepdims=True).astype(jnp.int32)
        hits = slot_numbers == named * capacity + position
        weights = weights + jnp.where(hits, probs[k : k + 1, :], 0.0)
        chosen = chosen + hits.astype(F32)
        taken = taken + jnp.sum(onehot, axis=1, keepdims=True)
    combine[...] = weights
    outgoing[...] = lax.dot_general(
        chosen.astype(BF16), tokens[...], (((1,), (1,)), ((), ())), preferred_element_type=F32
    ).astype(BF16)


def dispatched(ids, probs, tokens, experts, capacity):
    cols, rows = tokens.shape
    return pl.pallas_call(
        functools.partial(dispatch_kernel, experts, capacity),
        out_shape=(
            jax.ShapeDtypeStruct((experts * capacity, cols), BF16),
            jax.ShapeDtypeStruct((experts * capacity, rows), F32),
        ),
        name="dispatch",
    )(ids, probs, tokens)


IN_HBM = pl.BlockSpec(memory_space=pl.ANY)
IN_VMEM = pl.BlockSpec(memory_space=pltpu.MemorySpace.VMEM)


def laid_out(form, cols, sources, out, held, pieces, arrived, gone):
    each = CHUNK // cols
    steps = pieces.shape[0] // each
    reads = [
        [
            pltpu.make_async_copy(
                source.at[:, step * CHUNK : (step + 1) * CHUNK],
                held.at[i, :, step * CHUNK : (step + 1) * CHUNK],
                arrived.at[i, step],
            )
            for i, source in enumerate(sources)
        ]
        for step in range(steps)
    ]
    writes = [
        pltpu.make_async_copy(
            pieces.at[step * each : (step + 1) * each],
            out.at[step * each : (step + 1) * each],
            gone.at[step],
        )
        for step in range(steps)
    ]
    for row in reads:
        for copy in row:
            copy.start()
    for step in range(steps):
        for copy in reads[step]:
            copy.wait()
        for i in range(step * each, (step + 1) * each):
            pieces[i] = form(held, slice(i * cols, (i + 1) * cols))
        writes[step].start()
    for copy in writes:
        copy.wait()


def down_weights_kernel(cols, down, out, held, pieces, arrived, gone):
    def form(held, at):
        return held[0, :, at].astype(F32).T.astype(BF16)

    laid_out(form, cols, [down], out, held, pieces, arrived, gone)


def layout_call(kernel, name, cols, piece, sources, gain=()):
    units, width = sources[0].shape
    shape = (width // cols,) + piece
    return pl.pallas_call(
        functools.partial(kernel, cols),
        out_shape=jax.ShapeDtypeStruct(shape, BF16),
        in_specs=[IN_VMEM] * len(gain) + [IN_HBM] * len(sources),
        out_specs=IN_HBM,
        scratch_shapes=[
            pltpu.VMEM((len(sources), units, width), BF16),
            pltpu.VMEM(shape, BF16),
            pltpu.SemaphoreType.DMA((len(sources), width // CHUNK)),
            pltpu.SemaphoreType.DMA((width // CHUNK,)),
        ],
        compiler_params=pltpu.CompilerParams(vmem_limit_bytes=MOST),
        cost_estimate=SMALL,
        name=name,
    )(*gain, *sources)


def both_up_kernel(cols, gain, *refs):
    sources, outs, held, pieces, arrived, gone = refs[:4], refs[4:6], *refs[6:]
    each = CHUNK // cols
    steps = held.shape[2] // CHUNK
    reads = [
        [
            pltpu.make_async_copy(
                source.at[:, step * CHUNK : (step + 1) * CHUNK],
                held.at[i, :, step * CHUNK : (step + 1) * CHUNK],
                arrived.at[i, step],
            )
            for i, source in enumerate(sources)
        ]
        for step in range(steps)
    ]
    for row in reads:
        for copy in row:
            copy.start()
    writes = []
    for step in range(steps):
        for j, out in enumerate(outs):
            for copy in reads[step][2 * j : 2 * j + 2]:
                copy.wait()
            for i in range(step * each, (step + 1) * each):
                at = slice(i * cols, (i + 1) * cols)
                both = jnp.concatenate(
                    [held[2 * j, :, at].astype(F32), held[2 * j + 1, :, at].astype(F32)], axis=0
                )
                pieces[j, i] = (both * gain[:, at]).astype(BF16)
            write = pltpu.make_async_copy(
                pieces.at[j, step * each : (step + 1) * each],
                out.at[step * each : (step + 1) * each],
                gone.at[j, step],
            )
            write.start()
            writes.append(write)
    for copy in writes:
        copy.wait()


def up_weights(gain, dense_gate, dense_up, expert_gate, expert_up, cols):
    units, width = dense_gate.shape
    shape = (width // cols, 2 * units, cols)
    return pl.pallas_call(
        functools.partial(both_up_kernel, cols),
        out_shape=[jax.ShapeDtypeStruct(shape, BF16)] * 2,
        in_specs=[IN_VMEM] + [IN_HBM] * 4,
        out_specs=[IN_HBM] * 2,
        scratch_shapes=[
            pltpu.VMEM((4, units, width), BF16),
            pltpu.VMEM((2,) + shape, BF16),
            pltpu.SemaphoreType.DMA((4, width // CHUNK)),
            pltpu.SemaphoreType.DMA((2, width // CHUNK)),
        ],
        compiler_params=pltpu.CompilerParams(vmem_limit_bytes=MOST),
        cost_estimate=SMALL,
        name="up_weights",
    )(gain, dense_gate, dense_up, expert_gate, expert_up)


def down_weights(down, cols):
    return layout_call(down_weights_kernel, "down_weights", cols, (cols, down.shape[0]), [down])


def arrive_kernel(dense_rows, count, start, last, width, place, *refs):
    stacks, dense, routed = (refs[i * count : (i + 1) * count] for i in range(3))
    refs = refs[3 * count :]
    if not start:
        carried, refs = refs[:3], refs[3:]
    if last:
        hidden, refs = refs[0], refs[1:]
    dense_sum, routed_sum, squares = refs

    @pl.when(pl.program_id(0) == 0)
    def _():
        for i, ref in enumerate(refs):
            ref[...] = jnp.zeros_like(ref) if start else carried[i][...]

    for stack, dense_weight, routed_weight in zip(stacks, dense, routed):
        block = stack[0]
        dense_sum[...] += jnp.dot(
            dense_weight[0], block[:, :dense_rows], preferred_element_type=F32
        )
        routed_sum[...] += jnp.dot(
            routed_weight[0], block[:, dense_rows:], preferred_element_type=F32
        )
        values = block.astype(F32)
        values = values * values
        squares[...] += jnp.sum(values.reshape(values.shape[0] // 8, 8, values.shape[1]), axis=0)

    if last:

        @pl.when(pl.program_id(0) == pl.num_programs(0) - 1)
        def _():
            scale = lax.rsqrt(jnp.sum(squares[...], axis=0, keepdims=True) / width + 1e-05)
            units = dense_sum.shape[0] // 2
            for sums, span in (
                (dense_sum, slice(0, dense_rows)),
                (routed_sum, slice(dense_rows, scale.shape[1])),
            ):
                gates = sums[:units, :] * scale[:, span]
                ups = sums[units:, :] * scale[:, span]
                hidden[:, span] = (gates / (1.0 + jnp.exp(-gates)) * ups).astype(BF16)


def arrive(place, stage, weights, sums, dense_rows, last=False):
    count = len(stage)
    pieces, cols, rows = stage[0][0].shape
    height = weights[0].shape[1]
    start = sums is None

    def weight(outer, inner, other):
        def index(i, place):
            return piece_index(place, other, -1, outer, inner + i), 0, 0

        return pl.BlockSpec((1, height, cols), index)

    whole = lambda shape: pl.BlockSpec(shape, lambda i, place: (0, 0))
    shapes = [(height, dense_rows), (height, rows - dense_rows), (8, rows)]
    sum_specs = [whole(s) for s in shapes]
    if last:
        out_specs = whole((height // 2, rows))
        out_shape = jax.ShapeDtypeStruct((height // 2, rows), BF16)
        scratch = [pltpu.VMEM(s, F32) for s in shapes]
    else:
        out_specs, scratch = sum_specs, []
        out_shape = [jax.ShapeDtypeStruct(s, F32) for s in shapes]
    return pl.pallas_call(
        functools.partial(arrive_kernel, dense_rows, count, start, last, GROUP * cols),
        out_shape=out_shape,
        grid_spec=pltpu.PrefetchScalarGridSpec(
            num_scalar_prefetch=1,
            grid=(pieces,),
            in_specs=[pl.BlockSpec((1, cols, rows), lambda i, place: (i, 0, 0))] * count
            + [weight(*rest) for _, *rest in stage] * 2
            + ([] if start else sum_specs),
            out_specs=out_specs,
            scratch_shapes=scratch,
        ),
        compiler_params=pltpu.CompilerParams(vmem_limit_bytes=24 * MIB),
        cost_estimate=SMALL,
        name=f"arrive_{stage[-1][1]}_{count}",
    )(
        place,
        *[stack for stack, *_ in stage],
        *[weights[0]] * count,
        *[weights[1]] * count,
        *([] if start else sums),
    )


def down_kernel(dense_rows, place, hidden, *refs):
    mine, others = refs[4:]
    for out, dense, routed in ((mine, refs[0], refs[1]), (others, refs[2], refs[3])):
        for weight, span in (
            (dense, slice(0, dense_rows)),
            (routed, slice(dense_rows, hidden.shape[1])),
        ):
            out[0, :, span] = jnp.dot(
                weight[0], hidden[:, span], preferred_element_type=F32
            ).astype(out.dtype)


def down_pieces(place, hidden, weights, outer, dense_rows):
    units, rows = hidden.shape
    cols = weights[0].shape[1]

    def weight(other):
        def index(i, place):
            return piece_index(place, other, 1, outer, i), 0, 0

        return pl.BlockSpec((1, cols, units), index)

    out = pl.BlockSpec((1, cols, rows), lambda i, place: (i, 0, 0))
    shape = (SIDE, cols, rows)
    return pl.pallas_call(
        functools.partial(down_kernel, dense_rows),
        out_shape=(jax.ShapeDtypeStruct(shape, F32), jax.ShapeDtypeStruct(shape, BF16)),
        grid_spec=pltpu.PrefetchScalarGridSpec(
            num_scalar_prefetch=1,
            grid=(SIDE,),
            in_specs=[pl.BlockSpec((units, rows), lambda i, place: (0, 0))]
            + [weight(False)] * 2
            + [weight(True)] * 2,
            out_specs=(out, out),
        ),
        compiler_params=pltpu.CompilerParams(vmem_limit_bytes=16 * MIB),
        cost_estimate=SMALL,
        name=f"down_pieces_{outer}",
    )(place, hidden, weights[0], weights[1], weights[0], weights[1])


def shards(
    tokens,
    norm_gain,
    route_ids,
    route_probs,
    dense_gate,
    dense_up,
    dense_down,
    expert_gate,
    expert_up,
    expert_down,
):
    experts = lax.axis_size("expert")
    rows, choose = route_ids.shape
    cols = tokens.shape[1]
    capacity = 3 * rows * choose // (2 * experts)
    index = lax.axis_index("tensor")
    place = jnp.stack([index // (SIDE * PAIR), index // PAIR % SIDE, index % PAIR]).astype(jnp.int32)

    gain = norm_gain[None, :]

    outgoing, combine = dispatched(route_ids.T, route_probs.T, tokens.T, experts, capacity)
    received = lax.all_to_all(
        outgoing.reshape(experts, capacity, cols), "expert", 0, 0, tiled=True
    ).reshape(experts * capacity, cols)
    weights = up_weights(gain, dense_gate, dense_up, expert_gate[0], expert_up[0], cols)
    received, weights = lax.optimization_barrier((received, weights))
    own = jnp.concatenate([tokens.T, received.T], axis=1)

    def level_one(value, d):
        return lax.ppermute(value, "tensor", hops(d, True))

    def level_two(value, d):
        return lax.ppermute(value, "tensor", hops(d, False))

    arrived = [level_one(own, d) for d in range(1, SIDE)]
    routed_down = down_weights(expert_down[0], cols)
    arrived, routed_down = lax.optimization_barrier((arrived, routed_down))
    stack = jnp.stack([own] + arrived)
    near, far, left = [level_two(stack, d) for d in range(1, SIDE)]
    stack_other = sibling(stack)
    down = [down_weights(dense_down, cols), routed_down]
    add = functools.partial(arrive, place, weights=weights, dense_rows=rows)
    sums = add([(stack, 0, 0, False)], sums=None)
    near, stack_other, sums, down = lax.optimization_barrier((near, stack_other, sums, down))
    near_other = sibling(near)
    sums = add([(stack_other, 0, 0, True), (near, 1, 0, False)], sums=sums)
    far, left, sums = lax.optimization_barrier((far, left, sums))
    far_other, left_other = sibling(far), sibling(left)
    sums = add([(near_other, 1, 0, True), (far, 2, 0, False), (left, 3, 0, False)], sums=sums)
    far_other, left_other, sums = lax.optimization_barrier((far_other, left_other, sums))
    hidden = add([(far_other, 2, 0, True), (left_other, 3, 0, True)], sums=sums, last=True)

    pieces, order = {}, (2, 1, 3, 0)
    for i, outer in enumerate(order):
        mine, others = down_pieces(place, hidden, down, outer, rows)
        if i > 0:
            before = order[i - 1]
            pieces[before], hidden = lax.optimization_barrier((pieces[before], hidden))
        pieces[outer] = mine + sibling(others).astype(F32)
    level = pieces[0]
    for d in order[:-1]:
        level = level + level_two(pieces[d].astype(BF16), d).astype(F32)
    total = level[0]
    for d in order[:-1]:
        total = total + level_one(level[d].astype(BF16), d).astype(F32)

    back = total[:, rows:].astype(BF16).T.reshape(experts, capacity, cols)
    returned = lax.all_to_all(back, "expert", 0, 0, tiled=True).reshape(experts * capacity, cols)
    moe_out = jnp.dot(combine.T, returned.astype(F32), precision=lax.Precision.HIGHEST)
    return (total[:, :rows].T + moe_out).astype(BF16)


def solution(mesh):
    in_specs = (
        P("expert", "tensor"),
        P(),
        P("expert", None),
        P("expert", None),
        P("tensor", None),
        P("tensor", None),
        P("tensor", None),
        P("expert", "tensor", None),
        P("expert", "tensor", None),
        P("expert", "tensor", None),
    )
    out_specs = P("expert", "tensor")
    return jax.shard_map(shards, mesh=mesh, in_specs=in_specs, out_specs=out_specs, check_vma=False)
```
